32 devices in a mesh: groups: 2 (over y), seq: 8 (over z, x), tensor: 2 (over core).
Axes of the slice: x: 2, y: 2, z: 4, core: 2. Of those that a mesh axis runs over, the one named last changes fastest.
Arguments:
- inputs: bfloat16 [2048, 14336], P(('groups', 'seq'), 'tensor'), parts along dimension 0
- out_grads: bfloat16 [2048, 8192], P(('groups', 'seq'), 'tensor'), parts along dimension 0
- proj_in: bfloat16 [14336, 64], P('tensor'), may hold values from -0.046875 to 0.046875
- proj_out: bfloat16 [8192, 64], P('tensor'), may hold values from -0.0625 to 0.0625
- queries: bfloat16 [512, 4096], P(('groups', 'seq', 'tensor')), parts along dimension 0, may hold values from -6 to 6
- lengths: int32 [4], P('groups'), parts along dimension 0, may hold values from 1 to 512, 768 in all
Outputs:
- scores: float32 [512, 2], P(('groups', 'seq', 'tensor')), parts along dimension 0
The draws below stay inside these ranges and needn't reach their ends.
There are 2 independent parts, one for each index of `groups`. The reference program is written for one: setup_inputs(seed, part) draws one part's arguments, and reference() takes and returns one part's arrays. A program takes and returns all parts, laid end to end along the dimension named above; an argument that names none is the same for every part. Nothing has to cross between parts.
Inputs may be any that keep to these rules, and one draw needn't show every extreme that they name: lengths sum to 768.
All inputs are finite; a program needn't handle non-finite values.
Results may differ from the reference program's by a relative error of at most 0.035.
Values may be sent and summed in bfloat16 or wider, within the bound.
No kernel may reach another device: no remote copies, remote signals or barrier semaphores. Data moves between devices by JAX's collectives and lax.ppermute only.
A program may use at most 64 MiB of HBM per device.

```python
import math
import jax
import jax.numpy as jnp
import numpy as np
from jax import lax

D = 8192
FF = 14336
R = 64
NQ = 256
LEN = 512
SEQS = 2
TOKENS = 1024


def activations(key, rows, cols):
    keys = jax.random.split(key, 5)
    gauss = jax.random.normal(keys[0], (rows, cols), jnp.float32)
    noise = gauss
    colscale = jnp.exp(jax.random.uniform(keys[2], (cols,), jnp.float32, -0.7, 0.7))
    latent = jax.random.normal(keys[3], (rows, 3), jnp.float32)
    directions = jax.random.normal(keys[4], (3, cols), jnp.float32)
    shared = latent[:, 0:1] * directions[0] + latent[:, 1:2] * directions[1] + latent[:, 2:3] * directions[2]
    shared = shared * (1.5 / math.sqrt(3.0))
    ramp = jnp.sqrt(1.0 + 2.0 * jnp.arange(rows, dtype=jnp.float32) / (rows - 1))
    return ramp[:, None] * (noise * colscale + shared)


def draw_inputs(key, part):
    key = jax.random.fold_in(key, 7)
    return activations(key, TOKENS, FF).astype(jnp.bfloat16)


def draw_out_grads(key, part):
    key = jax.random.fold_in(key, 13)
    return activations(key, TOKENS, D).astype(jnp.bfloat16)


def levels(rng, extent, pieces, smallest, largest):
    gain = 1.0
    for position, blocks in pieces:
        heights = jax.random.uniform(jax.random.fold_in(jax.random.fold_in(rng, 6), position), (blocks,), jnp.float32, smallest / len(pieces), largest / len(pieces))
        gain = gain * jnp.repeat(jnp.exp(heights), extent[position] // blocks).reshape((-1,) + (1,) * (len(extent) - 1 - position))
    return gain


def profile(amount, total, most, skew):
    loads = [(1 << 20) // math.isqrt(grade ** skew) + 1 for grade in range(2, amount + 1)]
    spare, counts = total - most - (amount - 1), [1] * (amount - 1)
    while spare > 0:
        candidates = [i for i in range(amount - 1) if counts[i] < most]
        pool, budget = sum([loads[i] for i in candidates]), spare
        for i in candidates:
            extra = min(most - counts[i], max(1, budget * loads[i] // pool), spare)
            counts[i] = counts[i] + extra
            spare = spare - extra
    return np.array([most] + counts)


def uneven_parts(stream_key, amount, total, reach, skew):
    if amount == 2:
        one = jax.random.randint(stream_key, (), max(1, total - reach), min(reach, total - 1) + 1)
        return jnp.stack([one, total - one])
    sizes = jnp.asarray(profile(amount, total, reach, skew), jnp.int32)
    couples = (amount - 1) // 2
    donor, receiver = sizes[1:1 + 2 * couples:2], sizes[2:2 + 2 * couples:2]
    room = jnp.minimum(donor - 1, reach - receiver)
    moved = jax.random.randint(jax.random.fold_in(stream_key, 1), (couples,), 0, 1 << 20) % (room + 1)
    sizes = sizes.at[1:1 + 2 * couples:2].set(donor - moved).at[2:2 + 2 * couples:2].set(receiver + moved)
    return sizes[jax.random.permutation(jax.random.fold_in(stream_key, 2), amount)]


def normal_values(rng, dims, scale, limit, cuts=(), kind=jnp.bfloat16):
    drawn = scale * jax.random.normal(rng, dims, jnp.float32)
    if cuts:
        drawn = drawn * levels(rng, dims, cuts, -0.22, 0.18)
    return jnp.clip(drawn, -limit, limit).astype(kind)


def setup_inputs(seed: int = 0, part: int = 0) -> dict:
    streams_of = jax.random.split(jax.random.key(seed), 7)
    part_splits = jax.random.split(jax.random.fold_in(streams_of[6], part), 7)
    return {
        "inputs": draw_inputs(jax.random.fold_in(jax.random.fold_in(streams_of[6], part), 71), part),
        "out_grads": draw_out_grads(jax.random.fold_in(jax.random.fold_in(streams_of[6], part), 71), part),
        "proj_in": normal_values(streams_of[2], (FF, R), FF ** -0.5, 0.046875, ((0, 2),)),
        "proj_out": normal_values(streams_of[3], (D, R), D ** -0.5, 0.0625, ((0, 2),)),
        "queries": normal_values(part_splits[4], (NQ, R * R), 1.0, 6.0, ((0, 16),)),
        "lengths": uneven_parts(part_splits[5], SEQS, 3 * SEQS * LEN // 4, LEN, 2).astype(jnp.int32),
    }


damping = 0.1

def factor_inverse(moment, total, width):
    eye_mat = jnp.eye(width, dtype=jnp.float32)
    matrix = moment / total + damping * eye_mat
    lower = jnp.linalg.cholesky(matrix)
    return jax.scipy.linalg.cho_solve((lower, True), eye_mat)

def precondition(query_rows, inverse_out, inverse_in):
    width = inverse_in.shape[0]
    square = query_rows.astype(jnp.float32).reshape(query_rows.shape[0], width, width)
    mixed = jnp.einsum('ij,qjk,kl->qil', inverse_out, square, inverse_in, precision=lax.Precision.HIGHEST)
    return mixed.reshape(query_rows.shape[0], width * width).astype(jnp.bfloat16)

def reference(inputs, out_grads, proj_in, proj_out, queries, lengths):
    proj_x = jnp.dot(inputs.astype(jnp.float32), proj_in.astype(jnp.float32), preferred_element_type=jnp.float32)
    proj_g = jnp.dot(out_grads.astype(jnp.float32), proj_out.astype(jnp.float32), preferred_element_type=jnp.float32)
    positions = jnp.arange(TOKENS, dtype=jnp.int32)
    valid = (positions % LEN < lengths[positions // LEN]).astype(jnp.float32)[:, None]
    total = jnp.sum(lengths).astype(jnp.float32)
    masked_x = proj_x * valid
    masked_g = proj_g * valid
    moment_in = jnp.dot(masked_x.T, proj_x, precision=lax.Precision.HIGHEST)
    moment_out = jnp.dot(masked_g.T, proj_g, precision=lax.Precision.HIGHEST)
    inverse_in = factor_inverse(moment_in, total, R)
    inverse_out = factor_inverse(moment_out, total, R)
    precond = precondition(queries, inverse_out, inverse_in)
    grads = jnp.einsum('sti,stj->sij', masked_g.reshape(SEQS, LEN, R), proj_x.reshape(SEQS, LEN, R), precision=lax.Precision.HIGHEST)
    grads = grads.reshape(SEQS, R * R)
    scores = jnp.dot(precond.astype(jnp.float32), grads.T, precision=lax.Precision.HIGHEST)
    return scores / (R * math.sqrt(LEN))
```

```python
import functools
import math

import jax
import jax.numpy as jnp
from jax import lax
from jax.experimental import pallas as pl
from jax.experimental.pallas import tpu as pltpu
from jax.sharding import PartitionSpec as P

LEN = 512
DAMPING = 0.1
PANEL = 8
VMEM = pl.BlockSpec(memory_space=pltpu.VMEM)
HBM = pl.BlockSpec(memory_space=pltpu.HBM)
NT = (((1,), (1,)), ((), ()))
F32 = jnp.float32


def half(shape):
    return lax.broadcasted_iota(jnp.int32, shape, 1) < shape[1] // 2


def project(chunks, lengths, inputs, grads, proj_in, proj_out, out, *scratch):
    x_buf, g_buf, px_buf, pg_buf, count, sems = scratch
    width, tokens = px_buf.shape[0], x_buf.shape[0]
    jobs, sem = [], 0
    for rows, row_buf, mat, mat_buf, parts, lo in (
        (inputs, x_buf, proj_in, px_buf, chunks[0], 0),
        (grads, g_buf, proj_out, pg_buf, chunks[1], width),
    ):
        step = rows.shape[1] // parts
        for part in range(parts):
            cols = pl.ds(part * step, step)
            pair = []
            for src, dst in ((mat, mat_buf), (rows, row_buf)):
                pair.append(pltpu.make_async_copy(src.at[:, cols], dst.at[:, cols], sems.at[sem]))
                pair[-1].start()
                sem += 1
            jobs.append((pair, mat_buf, row_buf, cols, lo))
    scalars = pltpu.make_async_copy(lengths, count, sems.at[sem])
    scalars.start()
    totals = {}
    for pair, mat_buf, row_buf, cols, lo in jobs:
        for copy in pair:
            copy.wait()
        part = lax.dot_general(mat_buf[:, cols], row_buf[:, cols], NT, preferred_element_type=F32)
        totals[lo] = part if lo not in totals else totals[lo] + part
    scalars.wait()
    first = lax.axis_index("seq") * tokens
    valid = lax.broadcasted_iota(jnp.int32, (width, tokens), 1) + first % LEN < count[first // LEN]
    for lo, total in totals.items():
        out[lo : lo + width, :] = jnp.where(valid, total, 0.0)


def moments(tokens, mine, other, out):
    z = mine[...] + other[...]
    square = lax.dot_general(z, z, NT, preferred_element_type=F32, precision=lax.Precision.HIGHEST)
    width = square.shape[0] // 2
    top, bottom = square[:width], square[width:]
    left = half(top.shape)
    is_moment = lax.axis_index("tensor") == 1
    own = lax.axis_index("seq") * tokens // LEN
    twice = jnp.where(left, bottom, pltpu.roll(bottom, width, 1))
    for slab in range(out.shape[0]):
        side = jnp.where(left, 2 * slab, 2 * slab + 1)
        cross = jnp.where(side == own, twice, 0.0)
        moment = jnp.where(left, top, bottom) if slab == 0 else jnp.zeros_like(top)
        out[slab] = jnp.where(is_moment, moment, cross)


def invert(matrix):
    width = matrix.shape[0]
    blocks = width // 8
    lane = lax.broadcasted_iota(jnp.int32, (8, 2 * width), 1)
    row_of = lax.broadcasted_iota(jnp.int32, (8, 2 * width), 0)
    column = lane % width
    right = lane - column
    rows = [matrix[8 * b : 8 * b + 8] for b in range(blocks)]
    for panel in range(blocks):
        first = 8 * panel
        cols = []
        for t in range(8):
            index = right + (first + t)
            cols.append([jnp.take_along_axis(rows[b], index, axis=1) for b in range(blocks)])
        inside = (column >= first) & (column < first + 8)
        rows = [jnp.where(inside, 0.0, r) for r in rows]
        for t in range(8):
            unit = jnp.where(column[:1] == first + t, 1.0, 0.0)
            inverse = 1.0 / cols[t][panel][t : t + 1]
            pivot = (rows[panel][t : t + 1] + unit) * inverse
            for b in range(blocks):
                rows[b] = rows[b] - cols[t][b] * pivot
            rows[panel] = jnp.where(row_of == t, pivot, rows[panel])
            for j in range(t + 1, 8):
                scaled = cols[j][panel][t : t + 1] * inverse
                cols[j] = [cols[j][b] - cols[t][b] * scaled for b in range(blocks)]
                cols[j][panel] = jnp.where(row_of == t, scaled, cols[j][panel])
    return jnp.concatenate(rows, axis=0)


def inverses(total, mine, other, out):
    out[...] = mine[...] + other[...]

    @pl.when(lax.axis_index("tensor") == 1)
    def _():
        both = out[0]
        width = both.shape[0]
        lane = lax.broadcasted_iota(jnp.int32, both.shape, 1)
        row = lax.broadcasted_iota(jnp.int32, both.shape, 0)
        damped = both * (1.0 / total) + jnp.where(lane % width == row, DAMPING, 0.0)
        out[0] = invert(damped)


def score(scaling, mine, other, queries, out, weights):
    is_moment = lax.axis_index("tensor") == 1
    inv = jnp.where(is_moment, mine[0], other[0])
    width = inv.shape[0]
    inv_out = pltpu.roll(inv, width, 1)[:, :width]
    left = half(inv.shape)
    inv_twice = jnp.where(left, inv, pltpu.roll(inv, width, 1))
    upper = jnp.where(left, inv_twice, 0.0)
    lower = jnp.where(left, 0.0, inv_twice)
    diagonal = jnp.concatenate([upper, lower], axis=0)
    dot = functools.partial(jnp.dot, preferred_element_type=F32, precision=lax.Precision.HIGHEST)
    for slab in range(mine.shape[0]):
        grads = jnp.where(is_moment, other[slab], mine[slab])
        weights[...] = dot(dot(inv_out, grads), diagonal) * scaling
        even = weights[pl.ds(0, width // 2, 2), :]
        odd = weights[pl.ds(1, width // 2, 2), :]
        pair = left[: width // 2]
        flat = (
            jnp.where(pair, even, pltpu.roll(odd, width, 1)),
            jnp.where(pair, pltpu.roll(even, width, 1), odd),
        )
        sums = [jnp.zeros((queries.shape[0], 2 * width), F32) for _ in flat]
        for m in range(width // 2):
            block = queries[:, 2 * width * m : 2 * width * (m + 1)].astype(F32)
            for s in range(2):
                sums[s] = sums[s] + block * flat[s][m : m + 1]
        for s in range(2):
            if 2 * slab + s < out.shape[1]:
                out[:, 2 * slab + s : 2 * slab + s + 1] = jnp.sum(sums[s], axis=1, keepdims=True)


def swap(array):
    return lax.ppermute(array, "tensor", [(0, 1), (1, 0)])


def exchange(array, distance, devices):
    pairs = [(2 * i + c, 2 * (i ^ distance) + c) for i in range(devices) for c in range(2)]
    return lax.ppermute(array, ("seq", "tensor"), pairs)


def shards(inputs, out_grads, proj_in, proj_out, queries, lengths):
    width = proj_in.shape[1]
    tokens = inputs.shape[0]
    seq_count = lengths.shape[0]
    slabs = (seq_count + 1) // 2
    chunks = (4, 2)
    params = pltpu.CompilerParams(vmem_limit_bytes=16 << 20)
    partial_z = pl.pallas_call(
        functools.partial(project, chunks),
        out_shape=jax.ShapeDtypeStruct((2 * width, tokens), F32),
        in_specs=[HBM] * 5,
        out_specs=VMEM,
        scratch_shapes=[
            pltpu.VMEM(inputs.shape, inputs.dtype),
            pltpu.VMEM(out_grads.shape, out_grads.dtype),
            pltpu.VMEM(proj_in.shape[::-1], proj_in.dtype),
            pltpu.VMEM(proj_out.shape[::-1], proj_out.dtype),
            pltpu.SMEM(lengths.shape, lengths.dtype),
            pltpu.SemaphoreType.DMA((2 * sum(chunks) + 1,)),
        ],
        compiler_params=params,
        name="project",
    )(lengths, inputs, out_grads, proj_in.T, proj_out.T)
    payload_shape = jax.ShapeDtypeStruct((slabs, width, 2 * width), F32)
    payload = pl.pallas_call(
        functools.partial(moments, tokens),
        out_shape=payload_shape,
        in_specs=[VMEM] * 2,
        out_specs=VMEM,
        compiler_params=params,
        name="moments",
    )(partial_z, swap(partial_z))
    devices = lax.axis_size("seq")
    distance = 1
    while 2 * distance < devices:
        payload = payload + exchange(payload, distance, devices)
        distance *= 2
    total = 3 * seq_count * LEN // 4
    ready = pl.pallas_call(
        functools.partial(inverses, float(total)),
        out_shape=payload_shape,
        in_specs=[VMEM] * 2,
        out_specs=VMEM,
        compiler_params=params,
        name="inverses",
    )(payload, exchange(payload, distance, devices))
    scaling = 1.0 / (width * math.sqrt(LEN))
    return pl.pallas_call(
        functools.partial(score, scaling),
        out_shape=jax.ShapeDtypeStruct((queries.shape[0], seq_count), F32),
        in_specs=[VMEM] * 3,
        out_specs=VMEM,
        scratch_shapes=[pltpu.VMEM((width, 2 * width), F32)],
        compiler_params=params,
        name="score",
    )(ready, swap(ready), queries)


def solution(mesh):
    placed = (
        P(("groups", "seq"), "tensor"),
        P(("groups", "seq"), "tensor"),
        P("tensor", None),
        P("tensor", None),
        P(("groups", "seq", "tensor"), None),
        P("groups"),
    )
    return jax.shard_map(
        shards,
        mesh=mesh,
        in_specs=placed,
        out_specs=P(("groups", "seq", "tensor"), None),
        check_vma=False,
    )
```

```python
import functools
import math

import jax
import jax.numpy as jnp
from jax import lax
from jax.experimental import pallas as pl
from jax.experimental.pallas import tpu as pltpu
from jax.sharding import PartitionSpec as P

LEN = 512
DAMPING = 0.1
PANEL = 8
VMEM = pl.BlockSpec(memory_space=pltpu.VMEM)
HBM = pl.BlockSpec(memory_space=pltpu.HBM)
NT = (((1,), (1,)), ((), ()))
F32 = jnp.float32


def half(shape):
    return lax.broadcasted_iota(jnp.int32, shape, 1) < shape[1] // 2


def project(chunks, lengths, inputs, grads, proj_in, proj_out, out, *scratch):
    x_buf, g_buf, px_buf, pg_buf, count, sems = scratch
    width, tokens = px_buf.shape[0], x_buf.shape[0]
    jobs, sem = [], 0
    for rows, row_buf, mat, mat_buf, parts, lo in (
        (inputs, x_buf, proj_in, px_buf, chunks[0], 0),
        (grads, g_buf, proj_out, pg_buf, chunks[1], width),
    ):
        step = rows.shape[1] // parts
        for part in range(parts):
            cols = pl.ds(part * step, step)
            pair = []
            for src, dst in ((mat, mat_buf), (rows, row_buf)):
                pair.append(pltpu.make_async_copy(src.at[:, cols], dst.at[:, cols], sems.at[sem]))
                pair[-1].start()
                sem += 1
            jobs.append((pair, mat_buf, row_buf, cols, lo))
    scalars = pltpu.make_async_copy(lengths, count, sems.at[sem])
    scalars.start()
    totals = {}
    for pair, mat_buf, row_buf, cols, lo in jobs:
        for copy in pair:
            copy.wait()
        part = lax.dot_general(mat_buf[:, cols], row_buf[:, cols], NT, preferred_element_type=F32)
        totals[lo] = part if lo not in totals else totals[lo] + part
    scalars.wait()
    first = lax.axis_index("seq") * tokens
    valid = lax.broadcasted_iota(jnp.int32, (width, tokens), 1) + first % LEN < count[first // LEN]
    for lo, total in totals.items():
        out[lo : lo + width, :] = jnp.where(valid, total, 0.0)


def moments(tokens, mine, other, out):
    z = mine[...] + other[...]
    square = lax.dot_general(z, z, NT, preferred_element_type=F32, precision=lax.Precision.HIGHEST)
    width = square.shape[0] // 2
    top, bottom = square[:width], square[width:]
    left = half(top.shape)
    is_moment = lax.axis_index("tensor") == 1
    own = lax.axis_index("seq") * tokens // LEN
    twice = jnp.where(left, bottom, pltpu.roll(bottom, width, 1))
    for slab in range(out.shape[0]):
        side = jnp.where(left, 2 * slab, 2 * slab + 1)
        cross = jnp.where(side == own, twice, 0.0)
        moment = jnp.where(left, top, bottom) if slab == 0 else jnp.zeros_like(top)
        out[slab] = jnp.where(is_moment, moment, cross)


def invert(matrix):
    width = matrix.shape[0]
    blocks = width // 8
    lane = lax.broadcasted_iota(jnp.int32, (8, 2 * width), 1)
    row_of = lax.broadcasted_iota(jnp.int32, (8, 2 * width), 0)
    column = lane % width
    right = lane - column
    rows = [matrix[8 * b : 8 * b + 8] for b in range(blocks)]
    for panel in range(blocks):
        first = 8 * panel
        cols = []
        for t in range(8):
            index = right + (first + t)
            cols.append([jnp.take_along_axis(rows[b], index, axis=1) for b in range(blocks)])
        inside = (column >= first) & (column < first + 8)
        rows = [jnp.where(inside, 0.0, r) for r in rows]
        for t in range(8):
            unit = jnp.where(column[:1] == first + t, 1.0, 0.0)
            inverse = 1.0 / cols[t][panel][t : t + 1]
            pivot = (rows[panel][t : t + 1] + unit) * inverse
            for b in range(blocks):
                rows[b] = rows[b] - cols[t][b] * pivot
            rows[panel] = jnp.where(row_of == t, pivot, rows[panel])
            for j in range(t + 1, 8):
                scaled = cols[j][panel][t : t + 1] * inverse
                cols[j] = [cols[j][b] - cols[t][b] * scaled for b in range(blocks)]
                cols[j][panel] = jnp.where(row_of == t, scaled, cols[j][panel])
    return jnp.concatenate(rows, axis=0)


def inverses(total, mine, other, out):
    out[...] = mine[...] + other[...]

    @pl.when(lax.axis_index("tensor") == 1)
    def _():
        both = out[0]
        width = both.shape[0]
        lane = lax.broadcasted_iota(jnp.int32, both.shape, 1)
        row = lax.broadcasted_iota(jnp.int32, both.shape, 0)
        damped = both * (1.0 / total) + jnp.where(lane % width == row, DAMPING, 0.0)
        out[0] = invert(damped)


def score(scaling, mine, other, queries, out, weights):
    is_moment = lax.axis_index("tensor") == 1
    inv = jnp.where(is_moment, mine[0], other[0])
    width = inv.shape[0]
    inv_out = pltpu.roll(inv, width, 1)[:, :width]
    left = half(inv.shape)
    inv_twice = jnp.where(left, inv, pltpu.roll(inv, width, 1))
    upper = jnp.where(left, inv_twice, 0.0)
    lower = jnp.where(left, 0.0, inv_twice)
    diagonal = jnp.concatenate([upper, lower], axis=0)
    dot = functools.partial(jnp.dot, preferred_element_type=F32, precision=lax.Precision.HIGHEST)
    for slab in range(mine.shape[0]):
        grads = jnp.where(is_moment, other[slab], mine[slab])
        weights[...] = dot(dot(inv_out, grads), diagonal) * scaling
        even = weights[pl.ds(0, width // 2, 2), :]
        odd = weights[pl.ds(1, width // 2, 2), :]
        pair = left[: width // 2]
        flat = (
            jnp.where(pair, even, pltpu.roll(odd, width, 1)),
            jnp.where(pair, pltpu.roll(even, width, 1), odd),
        )
        sums = [jnp.zeros((queries.shape[0], 2 * width), F32) for _ in flat]
        for m in range(width // 2):
            block = queries[:, 2 * width * m : 2 * width * (m + 1)].astype(F32)
            for s in range(2):
                sums[s] = sums[s] + block * flat[s][m : m + 1]
        for s in range(2):
            if 2 * slab + s < out.shape[0]:
                ones = jnp.ones((8, 2 * width), F32)
                total = lax.dot_general(
                    ones, sums[s], NT, preferred_element_type=F32, precision=lax.Precision.HIGHEST
                )
                out[2 * slab + s : 2 * slab + s + 1, :] = total[:1]


def stay(array):
    return pltpu.with_memory_space_constraint(array, pltpu.HBM)


def swap(array):
    return lax.ppermute(array, "tensor", [(0, 1), (1, 0)])


def exchange(array, distance, devices):
    pairs = [(2 * i + c, 2 * (i ^ distance) + c) for i in range(devices) for c in range(2)]
    return lax.ppermute(array, ("seq", "tensor"), pairs)


def shards(inputs, out_grads, proj_in, proj_out, queries, lengths):
    width = proj_in.shape[1]
    tokens = inputs.shape[0]
    seq_count = lengths.shape[0]
    slabs = (seq_count + 1) // 2
    chunks = (4, 2)
    params = pltpu.CompilerParams(vmem_limit_bytes=16 << 20)
    partial_z = pl.pallas_call(
        functools.partial(project, chunks),
        out_shape=jax.ShapeDtypeStruct((2 * width, tokens), F32),
        in_specs=[HBM] * 5,
        out_specs=VMEM,
        scratch_shapes=[
            pltpu.VMEM(inputs.shape, inputs.dtype),
            pltpu.VMEM(out_grads.shape, out_grads.dtype),
            pltpu.VMEM(proj_in.shape[::-1], proj_in.dtype),
            pltpu.VMEM(proj_out.shape[::-1], proj_out.dtype),
            pltpu.SMEM(lengths.shape, lengths.dtype),
            pltpu.SemaphoreType.DMA((2 * sum(chunks) + 1,)),
        ],
        compiler_params=params,
        name="project",
    )(*map(stay, (lengths, inputs, out_grads, proj_in.T, proj_out.T)))
    payload_shape = jax.ShapeDtypeStruct((slabs, width, 2 * width), F32)
    payload = pl.pallas_call(
        functools.partial(moments, tokens),
        out_shape=payload_shape,
        in_specs=[VMEM] * 2,
        out_specs=VMEM,
        compiler_params=params,
        name="moments",
    )(partial_z, swap(partial_z))
    devices = lax.axis_size("seq")
    distance = 1
    while 2 * distance < devices:
        payload = payload + exchange(payload, distance, devices)
        distance *= 2
    total = 3 * seq_count * LEN // 4
    ready = pl.pallas_call(
        functools.partial(inverses, float(total)),
        out_shape=payload_shape,
        in_specs=[VMEM] * 2,
        out_specs=VMEM,
        compiler_params=params,
        name="inverses",
    )(payload, exchange(payload, distance, devices))
    scaling = 1.0 / (width * math.sqrt(LEN))
    scores = pl.pallas_call(
        functools.partial(score, scaling),
        out_shape=jax.ShapeDtypeStruct((seq_count, queries.shape[0]), F32),
        in_specs=[VMEM] * 3,
        out_specs=VMEM,
        scratch_shapes=[pltpu.VMEM((width, 2 * width), F32)],
        compiler_params=params,
        name="score",
    )(ready, swap(ready), queries)
    return scores.T


def solution(mesh):
    placed = (
        P(("groups", "seq"), "tensor"),
        P(("groups", "seq"), "tensor"),
        P("tensor", None),
        P("tensor", None),
        P(("groups", "seq", "tensor"), None),
        P("groups"),
    )
    return jax.shard_map(
        shards,
        mesh=mesh,
        in_specs=placed,
        out_specs=P(("groups", "seq", "tensor"), None),
        check_vma=False,
    )
```

```python
import functools
import math

import jax
import jax.numpy as jnp
from jax import lax
from jax.experimental import pallas as pl
from jax.experimental.pallas import tpu as pltpu
from jax.sharding import PartitionSpec as P

LEN = 512
DAMPING = 0.1
VMEM = pl.BlockSpec(memory_space=pltpu.VMEM)
HBM = pl.BlockSpec(memory_space=pltpu.HBM)
NT = (((1,), (1,)), ((), ()))
F32 = jnp.float32


def project(chunks, lengths, inputs, grads, proj_in, proj_out, out, *scratch):
    x_buf, g_buf, px_buf, pg_buf, count, sems = scratch
    width, tokens = px_buf.shape[0], x_buf.shape[0]
    jobs, sem = [], 0
    for rows, row_buf, mat, mat_buf, parts, lo in (
        (inputs, x_buf, proj_in, px_buf, chunks[0], 0),
        (grads, g_buf, proj_out, pg_buf, chunks[1], width),
    ):
        step = rows.shape[1] // parts
        for part in range(parts):
            cols = pl.ds(part * step, step)
            pair = []
            for src, dst in ((mat, mat_buf), (rows, row_buf)):
                pair.append(pltpu.make_async_copy(src.at[:, cols], dst.at[:, cols], sems.at[sem]))
                pair[-1].start()
                sem += 1
            jobs.append((pair, mat_buf, row_buf, cols, lo))
    scalars = pltpu.make_async_copy(lengths, count, sems.at[sem])
    scalars.start()
    totals = {}
    for pair, mat_buf, row_buf, cols, lo in jobs:
        for copy in pair:
            copy.wait()
        part = lax.dot_general(mat_buf[:, cols], row_buf[:, cols], NT, preferred_element_type=F32)
        totals[lo] = part if lo not in totals else totals[lo] + part
    scalars.wait()
    first = lax.axis_index("seq") * tokens
    valid = lax.broadcasted_iota(jnp.int32, (width, tokens), 1) + first % LEN < count[first // LEN]
    for lo, total in totals.items():
        out[lo : lo + width, :] = jnp.where(valid, total, 0.0)


def moments(mine, other, out):
    out[...] = jnp.zeros_like(out)

    @pl.when(lax.axis_index("tensor") == 1)
    def _():
        z = mine[...] + other[...]
        square = lax.dot_general(z, z, NT, preferred_element_type=F32, precision=lax.Precision.HIGHEST)
        width = square.shape[0] // 2
        top, bottom = square[:width], pltpu.roll(square[width:], width, 1)
        row = lax.broadcasted_iota(jnp.int32, top.shape, 0)
        lane = lax.broadcasted_iota(jnp.int32, top.shape, 1)
        out[0, :width] = jnp.where(lane < row, bottom, top)
        diagonal = jnp.sum(jnp.where(lane == row, bottom, 0.0), axis=0, keepdims=True)
        out[0, width : width + 1] = diagonal


def unpack(packed, diagonal):
    width = packed.shape[0]
    left = packed[:, :width]
    flipped = left.T
    row = lax.broadcasted_iota(jnp.int32, left.shape, 0)
    lane = lax.broadcasted_iota(jnp.int32, left.shape, 1)
    inner = jnp.where(lane < row, flipped, left)
    outer = jnp.where(lane < row, left, jnp.where(lane == row, diagonal[:, :width], flipped))
    return jnp.concatenate([inner, outer], axis=1)


def invert(matrix):
    width = matrix.shape[0]
    blocks = width // 8
    lane = lax.broadcasted_iota(jnp.int32, (8, 2 * width), 1)
    row_of = lax.broadcasted_iota(jnp.int32, (8, 2 * width), 0)
    column = lane % width
    right = lane - column
    rows = [matrix[8 * b : 8 * b + 8] for b in range(blocks)]
    for panel in range(blocks):
        first = 8 * panel
        cols = []
        for t in range(8):
            index = right + (first + t)
            cols.append([jnp.take_along_axis(rows[b], index, axis=1) for b in range(blocks)])
        inside = (column >= first) & (column < first + 8)
        rows = [jnp.where(inside, 0.0, r) for r in rows]
        for t in range(8):
            unit = jnp.where(column[:1] == first + t, 1.0, 0.0)
            inverse = 1.0 / cols[t][panel][t : t + 1]
            pivot = (rows[panel][t : t + 1] + unit) * inverse
            for b in range(blocks):
                rows[b] = rows[b] - cols[t][b] * pivot
            rows[panel] = jnp.where(row_of == t, pivot, rows[panel])
            for j in range(t + 1, 8):
                scaled = cols[j][panel][t : t + 1] * inverse
                cols[j] = [cols[j][b] - cols[t][b] * scaled for b in range(blocks)]
                cols[j][panel] = jnp.where(row_of == t, scaled, cols[j][panel])
    return jnp.concatenate(rows, axis=0)


def weigh(total, scaling, mine, other, out, rows):
    out[...] = jnp.zeros_like(out)

    @pl.when(lax.axis_index("tensor") == 1)
    def _():
        slabs, _, lanes = mine.shape
        width = lanes // 2
        packed = mine[0] + other[0]
        both = unpack(packed[:width], packed[width : width + 1])
        lane = lax.broadcasted_iota(jnp.int32, both.shape, 1)
        row = lax.broadcasted_iota(jnp.int32, both.shape, 0)
        inv = invert(both * (1.0 / total) + jnp.where(lane % width == row, DAMPING, 0.0))
        inv_in, inv_out = inv[:, :width], jnp.where(lane < width, 0.0, inv)
        exact = dict(preferred_element_type=F32, precision=lax.Precision.HIGHEST)
        devices = lax.axis_size("seq")
        upper = lax.axis_index("seq") // (devices // 2) == 1
        for slab in range(slabs):
            for high in (False, True):
                cross = jnp.where(upper == high, mine[slab, :width], other[slab, :width])
                part = lax.dot_general(inv_out, cross, NT, **exact)
                rows[...] = jnp.dot(part, inv_in, **exact) * scaling
                even, odd = rows[pl.ds(0, width // 2, 2), :], rows[pl.ds(1, width // 2, 2), :]
                out[slabs * high + slab] = jnp.concatenate([even, odd], axis=1)


def score(mine, other, queries, out):
    is_weight = lax.axis_index("tensor") == 1
    count, chunks, lanes = mine.shape
    ones = jnp.ones((8, lanes), F32)
    for s in range(count):
        weights = jnp.where(is_weight, mine[s], other[s])
        sums = jnp.zeros((queries.shape[0], lanes), F32)
        for m in range(chunks):
            sums = sums + queries[:, lanes * m : lanes * (m + 1)].astype(F32) * weights[m : m + 1]
        total = lax.dot_general(ones, sums, NT, preferred_element_type=F32, precision=lax.Precision.HIGHEST)
        out[s : s + 1, :] = total[:1]


def stay(array):
    return pltpu.with_memory_space_constraint(array, pltpu.HBM)


def swap(array):
    return lax.ppermute(array, "tensor", [(0, 1), (1, 0)])


def exchange(array, distance, groups, devices):
    near = 2 if distance == 1 else 1
    pairs = []
    for chip in range(groups * devices):
        pairs.append((2 * chip, 2 * (chip ^ near)))
        pairs.append((2 * chip + 1, 2 * (chip ^ distance) + 1))
    return lax.ppermute(array, ("groups", "seq", "tensor"), pairs)


def gather(mine, other, distance, width):
    high = lax.axis_index("seq") // distance % 2 == 1
    both = jnp.stack([jnp.where(high, other, mine), jnp.where(high, mine, other)])
    left = jnp.arange(mine.shape[-1]) < width
    return jnp.where(left, mine + other, both).reshape((-1,) + mine.shape[1:])


def shards(inputs, out_grads, proj_in, proj_out, queries, lengths):
    width = proj_in.shape[1]
    tokens = inputs.shape[0]
    seq_count = lengths.shape[0]
    chunks = (4, 2)
    params = pltpu.CompilerParams(vmem_limit_bytes=16 << 20)
    partial_z = pl.pallas_call(
        functools.partial(project, chunks),
        out_shape=jax.ShapeDtypeStruct((2 * width, tokens), F32),
        in_specs=[HBM] * 5,
        out_specs=VMEM,
        scratch_shapes=[
            pltpu.VMEM(inputs.shape, inputs.dtype),
            pltpu.VMEM(out_grads.shape, out_grads.dtype),
            pltpu.VMEM(proj_in.shape[::-1], proj_in.dtype),
            pltpu.VMEM(proj_out.shape[::-1], proj_out.dtype),
            pltpu.SMEM(lengths.shape, lengths.dtype),
            pltpu.SemaphoreType.DMA((2 * sum(chunks) + 1,)),
        ],
        compiler_params=params,
        name="project",
    )(*map(stay, (lengths, inputs, out_grads, proj_in.T, proj_out.T)))
    packed_rows = width + 8
    packed = pl.pallas_call(
        moments,
        out_shape=jax.ShapeDtypeStruct((1, packed_rows, 2 * width), F32),
        in_specs=[VMEM] * 2,
        out_specs=VMEM,
        compiler_params=params,
        name="moments",
    )(partial_z, swap(partial_z))
    groups, devices = lax.axis_size("groups"), lax.axis_size("seq")
    holders = devices // seq_count
    distance = 1
    while 2 * distance < devices:
        other = exchange(packed, distance, groups, devices)
        packed = packed + other if distance < holders else gather(packed, other, distance, width)
        distance *= 2
    total = 3 * seq_count * LEN // 4
    scaling = 1.0 / (width * math.sqrt(LEN))
    weights = pl.pallas_call(
        functools.partial(weigh, float(total), scaling),
        out_shape=jax.ShapeDtypeStruct((seq_count, width // 2, 2 * width), F32),
        in_specs=[VMEM] * 2,
        out_specs=VMEM,
        scratch_shapes=[pltpu.VMEM((width, width), F32)],
        compiler_params=params,
        name="weigh",
    )(packed, exchange(packed, distance, groups, devices))
    scores = pl.pallas_call(
        score,
        out_shape=jax.ShapeDtypeStruct((seq_count, queries.shape[0]), F32),
        in_specs=[VMEM] * 3,
        out_specs=VMEM,
        compiler_params=params,
        name="score",
    )(weights, swap(weights), queries)
    return scores.T


def solution(mesh):
    placed = (
        P(("groups", "seq"), "tensor"),
        P(("groups", "seq"), "tensor"),
        P("tensor", None),
        P("tensor", None),
        P(("groups", "seq", "tensor"), None),
        P("groups"),
    )
    return jax.shard_map(
        shards,
        mesh=mesh,
        in_specs=placed,
        out_specs=P(("groups", "seq", "tensor"), None),
        check_vma=False,
    )
```

```python
import functools
import math

import jax
import jax.numpy as jnp
from jax import lax
from jax.experimental import pallas as pl
from jax.experimental.pallas import tpu as pltpu
from jax.sharding import PartitionSpec as P

LEN = 512
DAMPING = 0.1
VMEM = pl.BlockSpec(memory_space=pltpu.VMEM)
HBM = pl.BlockSpec(memory_space=pltpu.HBM)
NN = (((1,), (0,)), ((), ()))
NT = (((1,), (1,)), ((), ()))
F32 = jnp.float32


def project(chunks, lengths, inputs, grads, proj_in, proj_out, out, *scratch):
    x_buf, g_buf, px_buf, pg_buf, count, sems = scratch
    width, tokens = px_buf.shape[0], x_buf.shape[0]
    jobs, sem = [], 0
    for rows, row_buf, mat, mat_buf, parts, lo in (
        (inputs, x_buf, proj_in, px_buf, chunks[0], 0),
        (grads, g_buf, proj_out, pg_buf, chunks[1], width),
    ):
        step = rows.shape[1] // parts
        for part in range(parts):
            cols = pl.ds(part * step, step)
            pair = []
            for src, dst in ((mat, mat_buf), (rows, row_buf)):
                pair.append(pltpu.make_async_copy(src.at[:, cols], dst.at[:, cols], sems.at[sem]))
                pair[-1].start()
                sem += 1
            jobs.append((pair, mat_buf, row_buf, cols, lo))
    scalars = pltpu.make_async_copy(lengths, count, sems.at[sem])
    scalars.start()
    totals = {}
    for pair, mat_buf, row_buf, cols, lo in jobs:
        for copy in pair:
            copy.wait()
        part = lax.dot_general(mat_buf[:, cols], row_buf[:, cols], NT, preferred_element_type=F32)
        totals[lo] = part if lo not in totals else totals[lo] + part
    scalars.wait()
    first = lax.axis_index("seq") * tokens
    valid = lax.broadcasted_iota(jnp.int32, (width, tokens), 1) + first % LEN < count[first // LEN]
    for lo, total in totals.items():
        out[lo : lo + width, :] = jnp.where(valid, total, 0.0)


def dot3(a, b, dims):
    halves = []
    for part in (a, b):
        high = part.astype(jnp.bfloat16)
        halves.append((high, (part - high.astype(F32)).astype(jnp.bfloat16)))
    (ah, al), (bh, bl) = halves
    dot = functools.partial(lax.dot_general, dimension_numbers=dims, preferred_element_type=F32)
    return dot(ah, bh) + (dot(ah, bl) + dot(al, bh))


def moments(mine, other, out):
    out[...] = jnp.zeros_like(out)

    @pl.when(lax.axis_index("tensor") == 1)
    def _():
        z = mine[...] + other[...]
        square = dot3(z, z, NT)
        width = square.shape[0] // 2
        top, bottom = square[:width], pltpu.roll(square[width:], width, 1)
        row = lax.broadcasted_iota(jnp.int32, top.shape, 0)
        lane = lax.broadcasted_iota(jnp.int32, top.shape, 1)
        out[0, :width] = jnp.where(lane < row, bottom, top)
        diagonal = jnp.sum(jnp.where(lane == row, bottom, 0.0), axis=0, keepdims=True)
        out[0, width : width + 1] = diagonal


def unpack(packed, diagonal):
    width = packed.shape[0]
    left = packed[:, :width]
    flipped = left.T
    row = lax.broadcasted_iota(jnp.int32, left.shape, 0)
    lane = lax.broadcasted_iota(jnp.int32, left.shape, 1)
    inner = jnp.where(lane < row, flipped, left)
    outer = jnp.where(lane < row, left, jnp.where(lane == row, diagonal[:, :width], flipped))
    return jnp.concatenate([inner, outer], axis=1)


def invert(state):
    width = state.shape[0]
    blocks = width // 8
    lane = lax.broadcasted_iota(jnp.int32, (8, 2 * width), 1)
    row_of = lax.broadcasted_iota(jnp.int32, (8, 2 * width), 0)
    column = lane % width
    right = lane - column

    def panel(step, carry):
        first = step * 8
        own = pl.ds(pl.multiple_of(first, 8), 8)
        inside = (column >= first) & (column < first + 8)
        index = [right + (first + t) for t in range(8)]
        rows = [state[8 * b : 8 * b + 8, :] for b in range(blocks)]
        pivots = state[own, :]
        heads = [jnp.take_along_axis(pivots, index[t], axis=1) for t in range(8)]
        cols = [[jnp.take_along_axis(r, index[t], axis=1) for r in rows] for t in range(8)]
        pivots = jnp.where(inside, jnp.where(column - first == row_of, 1.0, 0.0), pivots)
        rows = [jnp.where(inside, 0.0, r) for r in rows]
        for t in range(8):
            inverse = 1.0 / heads[t][t : t + 1]
            pivot = pivots[t : t + 1] * inverse
            here = row_of == t
            pivots = jnp.where(here, pivot, pivots - jnp.where(here, 0.0, heads[t]) * pivot)
            rows = [rows[b] - cols[t][b] * pivot for b in range(blocks)]
            for j in range(t + 1, 8):
                scaled = heads[j][t : t + 1] * inverse
                heads[j] = jnp.where(here, scaled, heads[j] - heads[t] * scaled)
                cols[j] = [cols[j][b] - cols[t][b] * scaled for b in range(blocks)]
        for b in range(blocks):
            state[8 * b : 8 * b + 8, :] = rows[b]
        state[own, :] = pivots
        return carry

    lax.fori_loop(0, blocks, panel, 0)


def inverses(total, mine, other, out):
    @pl.when(lax.axis_index("tensor") == 1)
    def _():
        width = out.shape[0]
        packed = mine[0] + other[0]
        both = unpack(packed[:width], packed[width : width + 1])
        lane = lax.broadcasted_iota(jnp.int32, both.shape, 1)
        row = lax.broadcasted_iota(jnp.int32, both.shape, 0)
        out[...] = both * (1.0 / total) + jnp.where(lane % width == row, DAMPING, 0.0)
        invert(out)


def weigh(scaling, inv, mine, other, out, rows):
    @pl.when(lax.axis_index("tensor") == 1)
    def _():
        slabs = mine.shape[0]
        width = inv.shape[0]
        lane = lax.broadcasted_iota(jnp.int32, inv.shape, 1)
        inv_in, inv_out = inv[:, :width], jnp.where(lane < width, 0.0, inv[...])
        exact = dict(preferred_element_type=F32, precision=lax.Precision.HIGHEST)
        devices = lax.axis_size("seq")
        upper = lax.axis_index("seq") // (devices // 2) == 1
        for slab in range(slabs):
            parts = []
            for high in (False, True):
                cross = jnp.where(upper == high, mine[slab, :width], other[slab, :width])
                parts.append(dot3(inv_out, cross, NT))
            rows[...] = dot3(jnp.concatenate(parts, axis=0), inv_in, NN) * scaling
            even, odd = rows[pl.ds(0, width, 2), :], rows[pl.ds(1, width, 2), :]
            both = jnp.concatenate([even, odd], axis=1)
            out[slab] = both[: width // 2]
            out[slabs + slab] = both[width // 2 :]


def score(mine, other, queries, out):
    is_weight = lax.axis_index("tensor") == 1
    count, chunks, lanes = mine.shape
    ones = jnp.ones((8, lanes), F32)
    for s in range(count):
        weights = jnp.where(is_weight, mine[s], other[s])
        sums = jnp.zeros((queries.shape[0], lanes), F32)
        for m in range(chunks):
            sums = sums + queries[:, lanes * m : lanes * (m + 1)].astype(F32) * weights[m : m + 1]
        total = lax.dot_general(ones, sums, NT, preferred_element_type=F32, precision=lax.Precision.HIGHEST)
        out[s : s + 1, :] = total[:1]


def stay(array):
    return pltpu.with_memory_space_constraint(array, pltpu.HBM)


def swap(array):
    return lax.ppermute(array, "tensor", [(0, 1), (1, 0)])


def exchange(array, distance, groups, devices):
    near = 2 if distance == 1 else 1
    pairs = []
    for chip in range(groups * devices):
        pairs.append((2 * chip, 2 * (chip ^ near)))
        pairs.append((2 * chip + 1, 2 * (chip ^ distance) + 1))
    return lax.ppermute(array, ("groups", "seq", "tensor"), pairs)


def gather(mine, other, distance, width):
    high = lax.axis_index("seq") // distance % 2 == 1
    both = jnp.stack([jnp.where(high, other, mine), jnp.where(high, mine, other)])
    left = jnp.arange(mine.shape[-1]) < width
    return jnp.where(left, mine + other, both).reshape((-1,) + mine.shape[1:])


def shards(inputs, out_grads, proj_in, proj_out, queries, lengths):
    width = proj_in.shape[1]
    tokens = inputs.shape[0]
    seq_count = lengths.shape[0]
    chunks = (4, 2)
    params = pltpu.CompilerParams(vmem_limit_bytes=16 << 20)
    partial_z = pl.pallas_call(
        functools.partial(project, chunks),
        out_shape=jax.ShapeDtypeStruct((2 * width, tokens), F32),
        in_specs=[HBM] * 5,
        out_specs=VMEM,
        scratch_shapes=[
            pltpu.VMEM(inputs.shape, inputs.dtype),
            pltpu.VMEM(out_grads.shape, out_grads.dtype),
            pltpu.VMEM(proj_in.shape[::-1], proj_in.dtype),
            pltpu.VMEM(proj_out.shape[::-1], proj_out.dtype),
            pltpu.SMEM(lengths.shape, lengths.dtype),
            pltpu.SemaphoreType.DMA((2 * sum(chunks) + 1,)),
        ],
        compiler_params=params,
        name="project",
    )(*map(stay, (lengths, inputs, out_grads, proj_in.T, proj_out.T)))
    packed_rows = width + 8
    packed = pl.pallas_call(
        moments,
        out_shape=jax.ShapeDtypeStruct((1, packed_rows, 2 * width), F32),
        in_specs=[VMEM] * 2,
        out_specs=VMEM,
        compiler_params=params,
        name="moments",
    )(partial_z, swap(partial_z))
    groups, devices = lax.axis_size("groups"), lax.axis_size("seq")
    holders = devices // seq_count
    distance = 1
    while 2 * distance < devices:
        other = exchange(packed, distance, groups, devices)
        packed = packed + other if distance < holders else gather(packed, other, distance, width)
        distance *= 2
    total = 3 * seq_count * LEN // 4
    scaling = 1.0 / (width * math.sqrt(LEN))
    other = exchange(packed, distance, groups, devices)
    inverse = pl.pallas_call(
        functools.partial(inverses, float(total)),
        out_shape=jax.ShapeDtypeStruct((width, 2 * width), F32),
        in_specs=[VMEM] * 2,
        out_specs=VMEM,
        compiler_params=params,
        name="inverses",
    )(packed, other)
    weights = pl.pallas_call(
        functools.partial(weigh, scaling),
        out_shape=jax.ShapeDtypeStruct((seq_count, width // 2, 2 * width), F32),
        in_specs=[VMEM] * 3,
        out_specs=VMEM,
        scratch_shapes=[pltpu.VMEM((2 * width, width), F32)],
        compiler_params=params,
        name="weigh",
    )(inverse, packed, other)
    scores = pl.pallas_call(
        score,
        out_shape=jax.ShapeDtypeStruct((seq_count, queries.shape[0]), F32),
        in_specs=[VMEM] * 3,
        out_specs=VMEM,
        compiler_params=params,
        name="score",
    )(weights, swap(weights), queries)
    return scores.T


def solution(mesh):
    placed = (
        P(("groups", "seq"), "tensor"),
        P(("groups", "seq"), "tensor"),
        P("tensor", None),
        P("tensor", None),
        P(("groups", "seq", "tensor"), None),
        P("groups"),
    )
    return jax.shard_map(
        shards,
        mesh=mesh,
        in_specs=placed,
        out_specs=P(("groups", "seq", "tensor"), None),
        check_vma=False,
    )
```

```python
import functools
import math

import jax
import jax.numpy as jnp
from jax import lax
from jax.experimental import pallas as pl
from jax.experimental.pallas import tpu as pltpu
from jax.sharding import PartitionSpec as P

LEN = 512
DAMPING = 0.1
VMEM = pl.BlockSpec(memory_space=pltpu.VMEM)
HBM = pl.BlockSpec(memory_space=pltpu.HBM)
NN = (((1,), (0,)), ((), ()))
NT = (((1,), (1,)), ((), ()))
F32 = jnp.float32


def split(lo, hi, parts, unit):
    units = (hi - lo) // unit
    edges = [lo + unit * -(-units * part // parts) for part in range(parts + 1)]
    return list(zip(edges, edges[1:]))


def project(spans, lengths, inputs, grads, proj_in, proj_out, out, buf, count, sems):
    width, tokens = proj_in.shape[0], inputs.shape[0]
    tile = 2 * tokens
    outer = grads.shape[1]
    x_rows, g_rows = pl.ds(width, tokens), pl.ds(width + tokens, tokens)
    px_rows, pg_rows = pl.ds(0, width), pl.ds(width + tile, width)
    for part, (lo, hi) in enumerate(spans):
        cols = pl.ds(lo, hi - lo)
        for src, rows in ((proj_in, px_rows), (inputs, x_rows), (grads, g_rows), (proj_out, pg_rows)):
            if lo < src.shape[1]:
                pltpu.make_async_copy(src.at[:, cols], buf.at[rows, cols], sems.at[part]).start()
    scalars = pltpu.make_async_copy(lengths, count, sems.at[len(spans)])
    scalars.start()

    def multiply(*accs):
        step = 0
        for part, (lo, hi) in enumerate(spans):
            rows = buf.shape[0] if lo < outer else width + tokens
            landed = buf.at[pl.ds(0, rows), pl.ds(lo, hi - lo)]
            pltpu.make_async_copy(landed, landed, sems.at[part]).wait()
            tiles = [pl.ds(start, tile) for start in range(lo, hi, tile)]
            if lo < outer:
                pairs = [((x_rows, px_rows, cols), (g_rows, pg_rows, cols)) for cols in tiles]
            else:
                pairs = [tuple((x_rows, px_rows, cols) for cols in tiles[i : i + 2]) for i in range(0, len(tiles), 2)]
            for pair in pairs:
                unit, stage = step % 2, step // 2 % 2
                step += 1
                blocks = [buf[rows, cols] for rows, _, cols in pair]
                both = jnp.concatenate(blocks * (2 // len(blocks)), axis=0)
                pltpu.matmul_push_rhs(both, stage, unit, transpose=True)
                for place, (rows, mat_rows, cols) in enumerate(pair):
                    acc = accs[2 * (place + (place == 1 and rows is x_rows)) + unit]
                    pltpu.matmul_acc_lhs(acc, buf[mat_rows, cols], load_staged_rhs=None if place else stage)
        scalars.wait()
        first = lax.axis_index("seq") * tokens
        valid = lax.broadcasted_iota(jnp.int32, (width, tokens), 1) + first % LEN < count[first // LEN]
        x_left, g_right, x_right = (
            pltpu.matmul_pop(accs[2 * kind]) + pltpu.matmul_pop(accs[2 * kind + 1]) for kind in range(3)
        )
        out[:width, :] = jnp.where(valid, x_left[:, :tokens] + x_right[:, tokens:], 0.0)
        out[width:, :] = jnp.where(valid, g_right[:, tokens:], 0.0)

    pl.run_scoped(multiply, *(pltpu.ACC(mxu_id=unit)((width, tile), F32) for unit in (0, 1, 0, 1, 0, 1)))


def dot3(a, b, dims):
    halves = []
    for part in (a, b):
        high = part.astype(jnp.bfloat16)
        halves.append((high, (part - high.astype(F32)).astype(jnp.bfloat16)))
    (ah, al), (bh, bl) = halves
    dot = functools.partial(lax.dot_general, dimension_numbers=dims, preferred_element_type=F32)
    return dot(ah, bh) + (dot(ah, bl) + dot(al, bh))


def moments(mine, other, out):
    out[...] = jnp.zeros_like(out)

    @pl.when(lax.axis_index("tensor") == 1)
    def _():
        z = mine[...] + other[...]
        square = dot3(z, z, NT)
        width = square.shape[0] // 2
        top, bottom = square[:width], pltpu.roll(square[width:], width, 1)
        row = lax.broadcasted_iota(jnp.int32, top.shape, 0)
        lane = lax.broadcasted_iota(jnp.int32, top.shape, 1)
        out[0, :width] = jnp.where(lane < row, bottom, top)
        diagonal = jnp.sum(jnp.where(lane == row, bottom, 0.0), axis=0, keepdims=True)
        out[0, width : width + 1] = diagonal


def unpack(packed, diagonal):
    width = packed.shape[0]
    left = packed[:, :width]
    flipped = left.T
    row = lax.broadcasted_iota(jnp.int32, left.shape, 0)
    lane = lax.broadcasted_iota(jnp.int32, left.shape, 1)
    inner = jnp.where(lane < row, flipped, left)
    outer = jnp.where(lane < row, left, jnp.where(lane == row, diagonal[:, :width], flipped))
    return jnp.concatenate([inner, outer], axis=1)


def invert(state):
    width = state.shape[0]
    blocks = width // 8
    lane = lax.broadcasted_iota(jnp.int32, (8, 2 * width), 1)
    row_of = lax.broadcasted_iota(jnp.int32, (8, 2 * width), 0)
    column = lane % width
    right = lane - column

    def panel(step, carry):
        first = step * 8
        own = pl.ds(pl.multiple_of(first, 8), 8)
        inside = (column >= first) & (column < first + 8)
        index = [right + (first + t) for t in range(8)]
        rows = [state[8 * b : 8 * b + 8, :] for b in range(blocks)]
        pivots = state[own, :]
        heads = [jnp.take_along_axis(pivots, index[t], axis=1) for t in range(8)]
        cols = [[jnp.take_along_axis(r, index[t], axis=1) for r in rows] for t in range(8)]
        pivots = jnp.where(inside, jnp.where(column - first == row_of, 1.0, 0.0), pivots)
        rows = [jnp.where(inside, 0.0, r) for r in rows]
        for t in range(8):
            inverse = 1.0 / heads[t][t : t + 1]
            pivot = pivots[t : t + 1] * inverse
            here = row_of == t
            pivots = jnp.where(here, pivot, pivots - jnp.where(here, 0.0, heads[t]) * pivot)
            rows = [rows[b] - cols[t][b] * pivot for b in range(blocks)]
            for j in range(t + 1, 8):
                scaled = heads[j][t : t + 1] * inverse
                heads[j] = jnp.where(here, scaled, heads[j] - heads[t] * scaled)
                cols[j] = [cols[j][b] - cols[t][b] * scaled for b in range(blocks)]
        for b in range(blocks):
            state[8 * b : 8 * b + 8, :] = rows[b]
        state[own, :] = pivots
        return carry

    lax.fori_loop(0, blocks, panel, 0)


def inverses(total, mine, other, out):
    @pl.when(lax.axis_index("tensor") == 1)
    def _():
        width = out.shape[0]
        packed = mine[0] + other[0]
        both = unpack(packed[:width], packed[width : width + 1])
        lane = lax.broadcasted_iota(jnp.int32, both.shape, 1)
        row = lax.broadcasted_iota(jnp.int32, both.shape, 0)
        out[...] = both * (1.0 / total) + jnp.where(lane % width == row, DAMPING, 0.0)
        invert(out)


def weigh(scaling, inv, mine, other, out, rows):
    @pl.when(lax.axis_index("tensor") == 1)
    def _():
        slabs = mine.shape[0]
        width = inv.shape[0]
        lane = lax.broadcasted_iota(jnp.int32, inv.shape, 1)
        inv_in, inv_out = inv[:, :width], jnp.where(lane < width, 0.0, inv[...])
        exact = dict(preferred_element_type=F32, precision=lax.Precision.HIGHEST)
        devices = lax.axis_size("seq")
        upper = lax.axis_index("seq") // (devices // 2) == 1
        for slab in range(slabs):
            parts = []
            for high in (False, True):
                cross = jnp.where(upper == high, mine[slab, :width], other[slab, :width])
                parts.append(dot3(inv_out, cross, NT))
            rows[...] = dot3(jnp.concatenate(parts, axis=0), inv_in, NN) * scaling
            even, odd = rows[pl.ds(0, width, 2), :], rows[pl.ds(1, width, 2), :]
            both = jnp.concatenate([even, odd], axis=1)
            out[slab] = both[: width // 2]
            out[slabs + slab] = both[width // 2 :]


def score(mine, other, queries, out):
    is_weight = lax.axis_index("tensor") == 1
    count, chunks, lanes = mine.shape
    ones = jnp.ones((8, lanes), F32)
    for s in range(count):
        weights = jnp.where(is_weight, mine[s], other[s])
        sums = jnp.zeros((queries.shape[0], lanes), F32)
        for m in range(chunks):
            sums = sums + queries[:, lanes * m : lanes * (m + 1)].astype(F32) * weights[m : m + 1]
        total = lax.dot_general(ones, sums, NT, preferred_element_type=F32, precision=lax.Precision.HIGHEST)
        out[s : s + 1, :] = total[:1]


def stay(array):
    return pltpu.with_memory_space_constraint(array, pltpu.HBM)


def swap(array):
    return lax.ppermute(array, "tensor", [(0, 1), (1, 0)])


def exchange(array, distance, groups, devices):
    near = 2 if distance == 1 else 1
    pairs = []
    for chip in range(groups * devices):
        pairs.append((2 * chip, 2 * (chip ^ near)))
        pairs.append((2 * chip + 1, 2 * (chip ^ distance) + 1))
    return lax.ppermute(array, ("groups", "seq", "tensor"), pairs)


def gather(mine, other, distance, width):
    high = lax.axis_index("seq") // distance % 2 == 1
    both = jnp.stack([jnp.where(high, other, mine), jnp.where(high, mine, other)])
    left = jnp.arange(mine.shape[-1]) < width
    return jnp.where(left, mine + other, both).reshape((-1,) + mine.shape[1:])


def shards(inputs, out_grads, proj_in, proj_out, queries, lengths):
    width = proj_in.shape[1]
    tokens = inputs.shape[0]
    seq_count = lengths.shape[0]
    inner, outer = inputs.shape[1], out_grads.shape[1]
    tile = 2 * tokens
    spans = split(outer, inner, 2, 2 * tile) + split(0, outer, 3, tile)
    params = pltpu.CompilerParams(vmem_limit_bytes=16 << 20)
    partial_z = pl.pallas_call(
        functools.partial(project, spans),
        out_shape=jax.ShapeDtypeStruct((2 * width, tokens), F32),
        in_specs=[HBM] * 5,
        out_specs=VMEM,
        scratch_shapes=[
            pltpu.VMEM((2 * (width + tokens), inner), inputs.dtype),
            pltpu.SMEM(lengths.shape, lengths.dtype),
            pltpu.SemaphoreType.DMA((len(spans) + 1,)),
        ],
        compiler_params=params,
        name="project",
    )(*map(stay, (lengths, inputs, out_grads, proj_in.T, proj_out.T)))
    packed_rows = width + 8
    packed = pl.pallas_call(
        moments,
        out_shape=jax.ShapeDtypeStruct((1, packed_rows, 2 * width), F32),
        in_specs=[VMEM] * 2,
        out_specs=VMEM,
        compiler_params=params,
        name="moments",
    )(partial_z, swap(partial_z))
    groups, devices = lax.axis_size("groups"), lax.axis_size("seq")
    holders = devices // seq_count
    distance = 1
    while 2 * distance < devices:
        other = exchange(packed, distance, groups, devices)
        packed = packed + other if distance < holders else gather(packed, other, distance, width)
        distance *= 2
    total = 3 * seq_count * LEN // 4
    scaling = 1.0 / (width * math.sqrt(LEN))
    other = exchange(packed, distance, groups, devices)
    inverse = pl.pallas_call(
        functools.partial(inverses, float(total)),
        out_shape=jax.ShapeDtypeStruct((width, 2 * width), F32),
        in_specs=[VMEM] * 2,
        out_specs=VMEM,
        compiler_params=params,
        name="inverses",
    )(packed, other)
    weights = pl.pallas_call(
        functools.partial(weigh, scaling),
        out_shape=jax.ShapeDtypeStruct((seq_count, width // 2, 2 * width), F32),
        in_specs=[VMEM] * 3,
        out_specs=VMEM,
        scratch_shapes=[pltpu.VMEM((2 * width, width), F32)],
        compiler_params=params,
        name="weigh",
    )(inverse, packed, other)
    scores = pl.pallas_call(
        score,
        out_shape=jax.ShapeDtypeStruct((seq_count, queries.shape[0]), F32),
        in_specs=[VMEM] * 3,
        out_specs=VMEM,
        compiler_params=params,
        name="score",
    )(weights, swap(weights), queries)
    return scores.T


def solution(mesh):
    placed = (
        P(("groups", "seq"), "tensor"),
        P(("groups", "seq"), "tensor"),
        P("tensor", None),
        P("tensor", None),
        P(("groups", "seq", "tensor"), None),
        P("groups"),
    )
    return jax.shard_map(
        shards,
        mesh=mesh,
        in_specs=placed,
        out_specs=P(("groups", "seq", "tensor"), None),
        check_vma=False,
    )
```

```python
import functools
import math

import jax
import jax.numpy as jnp
from jax import lax
from jax.experimental import pallas as pl
from jax.experimental.pallas import tpu as pltpu
from jax.sharding import PartitionSpec as P

LEN = 512
DAMPING = 0.1
PANEL = 16
VMEM = pl.BlockSpec(memory_space=pltpu.VMEM)
HBM = pl.BlockSpec(memory_space=pltpu.HBM)
NN = (((1,), (0,)), ((), ()))
NT = (((1,), (1,)), ((), ()))
F32 = jnp.float32


def split(lo, hi, parts, unit):
    units = (hi - lo) // unit
    edges = [lo + unit * -(-units * part // parts) for part in range(parts + 1)]
    return list(zip(edges, edges[1:]))


def project(spans, lengths, inputs, grads, proj_in, proj_out, out, buf, count, sems):
    width, tokens = proj_in.shape[0], inputs.shape[0]
    tile = 2 * tokens
    outer = grads.shape[1]
    x_rows, g_rows = pl.ds(width, tokens), pl.ds(width + tokens, tokens)
    px_rows, pg_rows = pl.ds(0, width), pl.ds(width + tile, width)
    for part, (lo, hi) in enumerate(spans):
        cols = pl.ds(lo, hi - lo)
        for src, rows in ((proj_in, px_rows), (inputs, x_rows), (grads, g_rows), (proj_out, pg_rows)):
            if lo < src.shape[1]:
                pltpu.make_async_copy(src.at[:, cols], buf.at[rows, cols], sems.at[part]).start()
    scalars = pltpu.make_async_copy(lengths, count, sems.at[len(spans)])
    scalars.start()

    def multiply(*accs):
        step = 0
        for part, (lo, hi) in enumerate(spans):
            rows = buf.shape[0] if lo < outer else width + tokens
            landed = buf.at[pl.ds(0, rows), pl.ds(lo, hi - lo)]
            pltpu.make_async_copy(landed, landed, sems.at[part]).wait()
            tiles = [pl.ds(start, tile) for start in range(lo, hi, tile)]
            if lo < outer:
                pairs = [((x_rows, px_rows, cols), (g_rows, pg_rows, cols)) for cols in tiles]
            else:
                pairs = [tuple((x_rows, px_rows, cols) for cols in tiles[i : i + 2]) for i in range(0, len(tiles), 2)]
            for pair in pairs:
                unit, stage = step % 2, step // 2 % 2
                step += 1
                blocks = [buf[rows, cols] for rows, _, cols in pair]
                both = jnp.concatenate(blocks * (2 // len(blocks)), axis=0)
                pltpu.matmul_push_rhs(both, stage, unit, transpose=True)
                for place, (rows, mat_rows, cols) in enumerate(pair):
                    acc = accs[2 * (place + (place == 1 and rows is x_rows)) + unit]
                    pltpu.matmul_acc_lhs(acc, buf[mat_rows, cols], load_staged_rhs=None if place else stage)
        scalars.wait()
        first = lax.axis_index("seq") * tokens
        valid = lax.broadcasted_iota(jnp.int32, (width, tokens), 1) + first % LEN < count[first // LEN]
        x_left, g_right, x_right = (
            pltpu.matmul_pop(accs[2 * kind]) + pltpu.matmul_pop(accs[2 * kind + 1]) for kind in range(3)
        )
        out[:width, :] = jnp.where(valid, x_left[:, :tokens] + x_right[:, tokens:], 0.0)
        out[width:, :] = jnp.where(valid, g_right[:, tokens:], 0.0)

    pl.run_scoped(multiply, *(pltpu.ACC(mxu_id=unit)((width, tile), F32) for unit in (0, 1, 0, 1, 0, 1)))


def dot3(a, b, dims):
    halves = []
    for part in (a, b):
        high = part.astype(jnp.bfloat16)
        halves.append((high, (part - high.astype(F32)).astype(jnp.bfloat16)))
    (ah, al), (bh, bl) = halves
    dot = functools.partial(lax.dot_general, dimension_numbers=dims, preferred_element_type=F32)
    return dot(ah, bh) + (dot(ah, bl) + dot(al, bh))


def moments(mine, other, out):
    out[...] = jnp.zeros_like(out)

    @pl.when(lax.axis_index("tensor") == 1)
    def _():
        z = mine[...] + other[...]
        square = dot3(z, z, NT)
        width = square.shape[0] // 2
        top, bottom = square[:width], pltpu.roll(square[width:], width, 1)
        row = lax.broadcasted_iota(jnp.int32, top.shape, 0)
        lane = lax.broadcasted_iota(jnp.int32, top.shape, 1)
        out[0, :width] = jnp.where(lane < row, bottom, top)
        diagonal = jnp.sum(jnp.where(lane == row, bottom, 0.0), axis=0, keepdims=True)
        out[0, width : width + 1] = diagonal


def unpack(packed, diagonal):
    width = packed.shape[0]
    left = packed[:, :width]
    flipped = left.T
    row = lax.broadcasted_iota(jnp.int32, left.shape, 0)
    lane = lax.broadcasted_iota(jnp.int32, left.shape, 1)
    inner = jnp.where(lane < row, flipped, left)
    outer = jnp.where(lane < row, left, jnp.where(lane == row, diagonal[:, :width], flipped))
    return jnp.concatenate([inner, outer], axis=1)


def invert(state):
    width = state.shape[0]
    lane = lax.broadcasted_iota(jnp.int32, (8, 2 * width), 1)
    row_of = lax.broadcasted_iota(jnp.int32, (8, 2 * width), 0)
    column = lane % width
    right = lane - column

    def panel(step, carry):
        first = step * PANEL
        own = pl.ds(pl.multiple_of(first, PANEL), PANEL)
        inside = (column >= first) & (column < first + PANEL)
        index = [right + (first + t) for t in range(PANEL)]
        block = state[own, :]
        pivots = [block[8 * i : 8 * i + 8] for i in range(PANEL // 8)]
        heads = [[jnp.take_along_axis(p, index[t], axis=1) for p in pivots] for t in range(PANEL)]
        rows = [state[8 * b : 8 * b + 8, :] for b in range(width // 8)]
        cols = [[jnp.take_along_axis(r, index[t], axis=1) for r in rows] for t in range(PANEL)]
        for i in range(PANEL // 8):
            unit = jnp.where(column - first == row_of + 8 * i, 1.0, 0.0)
            pivots[i] = jnp.where(inside, unit, pivots[i])
        for t in range(PANEL):
            at, sub = t // 8, t % 8
            here = row_of == sub
            inverse = 1.0 / heads[t][at][sub : sub + 1]
            rest = [jnp.where(here, 0.0, h) if i == at else h for i, h in enumerate(heads[t])]

            def step_rows(tiles):
                scaled = tiles[at][sub : sub + 1] * inverse
                return [(jnp.where(here, scaled, x) if i == at else x) - rest[i] * scaled for i, x in enumerate(tiles)]

            pivots = step_rows(pivots)
            heads[t + 1 :] = [step_rows(head) for head in heads[t + 1 :]]
        for b in range(width // 8):
            total = jnp.where(inside, 0.0, rows[b])
            for t in range(PANEL):
                total = total - cols[t][b] * pivots[t // 8][t % 8 : t % 8 + 1]
            state[8 * b : 8 * b + 8, :] = total
        state[own, :] = jnp.concatenate(pivots, axis=0)
        return carry

    lax.fori_loop(0, width // PANEL, panel, 0)


def inverses(total, mine, other, out):
    @pl.when(lax.axis_index("tensor") == 1)
    def _():
        width = out.shape[0]
        packed = mine[0] + other[0]
        both = unpack(packed[:width], packed[width : width + 1])
        lane = lax.broadcasted_iota(jnp.int32, both.shape, 1)
        row = lax.broadcasted_iota(jnp.int32, both.shape, 0)
        out[...] = both * (1.0 / total) + jnp.where(lane % width == row, DAMPING, 0.0)
        invert(out)


def weigh(scaling, inv, mine, other, out, rows):
    @pl.when(lax.axis_index("tensor") == 1)
    def _():
        slabs = mine.shape[0]
        width = inv.shape[0]
        lane = lax.broadcasted_iota(jnp.int32, inv.shape, 1)
        inv_in, inv_out = inv[:, :width], jnp.where(lane < width, 0.0, inv[...])
        exact = dict(preferred_element_type=F32, precision=lax.Precision.HIGHEST)
        devices = lax.axis_size("seq")
        upper = lax.axis_index("seq") // (devices // 2) == 1
        for slab in range(slabs):
            parts = []
            for high in (False, True):
                cross = jnp.where(upper == high, mine[slab, :width], other[slab, :width])
                parts.append(dot3(inv_out, cross, NT))
            rows[...] = dot3(jnp.concatenate(parts, axis=0), inv_in, NN) * scaling
            even, odd = rows[pl.ds(0, width, 2), :], rows[pl.ds(1, width, 2), :]
            both = jnp.concatenate([even, odd], axis=1)
            out[slab] = both[: width // 2]
            out[slabs + slab] = both[width // 2 :]


def score(mine, other, queries, out):
    is_weight = lax.axis_index("tensor") == 1
    count, chunks, lanes = mine.shape
    ones = jnp.ones((8, lanes), F32)
    for s in range(count):
        weights = jnp.where(is_weight, mine[s], other[s])
        sums = jnp.zeros((queries.shape[0], lanes), F32)
        for m in range(chunks):
            sums = sums + queries[:, lanes * m : lanes * (m + 1)].astype(F32) * weights[m : m + 1]
        total = lax.dot_general(ones, sums, NT, preferred_element_type=F32, precision=lax.Precision.HIGHEST)
        out[s : s + 1, :] = total[:1]


def stay(array):
    return pltpu.with_memory_space_constraint(array, pltpu.HBM)


def swap(array):
    return lax.ppermute(array, "tensor", [(0, 1), (1, 0)])


def exchange(array, distance, groups, devices):
    near = distance if distance < 4 else 1
    pairs = []
    for chip in range(groups * devices):
        pairs.append((2 * chip, 2 * (chip ^ near)))
        pairs.append((2 * chip + 1, 2 * (chip ^ distance) + 1))
    return lax.ppermute(array, ("groups", "seq", "tensor"), pairs)


def gather(mine, other, distance, width):
    high = lax.axis_index("seq") // distance % 2 == 1
    both = jnp.stack([jnp.where(high, other, mine), jnp.where(high, mine, other)])
    left = jnp.arange(mine.shape[-1]) < width
    return jnp.where(left, mine + other, both).reshape((-1,) + mine.shape[1:])


def shards(inputs, out_grads, proj_in, proj_out, queries, lengths):
    width = proj_in.shape[1]
    tokens = inputs.shape[0]
    seq_count = lengths.shape[0]
    inner, outer = inputs.shape[1], out_grads.shape[1]
    tile = 2 * tokens
    spans = split(outer, inner, 2, 2 * tile) + split(0, outer, 3, tile)
    params = pltpu.CompilerParams(vmem_limit_bytes=16 << 20)
    partial_z = pl.pallas_call(
        functools.partial(project, spans),
        out_shape=jax.ShapeDtypeStruct((2 * width, tokens), F32),
        in_specs=[HBM] * 5,
        out_specs=VMEM,
        scratch_shapes=[
            pltpu.VMEM((2 * (width + tokens), inner), inputs.dtype),
            pltpu.SMEM(lengths.shape, lengths.dtype),
            pltpu.SemaphoreType.DMA((len(spans) + 1,)),
        ],
        compiler_params=params,
        name="project",
    )(*map(stay, (lengths, inputs, out_grads, proj_in.T, proj_out.T)))
    packed_rows = width + 8
    packed = pl.pallas_call(
        moments,
        out_shape=jax.ShapeDtypeStruct((1, packed_rows, 2 * width), F32),
        in_specs=[VMEM] * 2,
        out_specs=VMEM,
        compiler_params=params,
        name="moments",
    )(partial_z, swap(partial_z))
    groups, devices = lax.axis_size("groups"), lax.axis_size("seq")
    holders = devices // seq_count
    packed = packed + sum(exchange(packed, near, groups, devices) for near in range(1, holders))
    distance = holders
    while 2 * distance < devices:
        packed = gather(packed, exchange(packed, distance, groups, devices), distance, width)
        distance *= 2
    total = 3 * seq_count * LEN // 4
    scaling = 1.0 / (width * math.sqrt(LEN))
    other = exchange(packed, distance, groups, devices)
    inverse = pl.pallas_call(
        functools.partial(inverses, float(total)),
        out_shape=jax.ShapeDtypeStruct((width, 2 * width), F32),
        in_specs=[VMEM] * 2,
        out_specs=VMEM,
        compiler_params=params,
        name="inverses",
    )(packed, other)
    weights = pl.pallas_call(
        functools.partial(weigh, scaling),
        out_shape=jax.ShapeDtypeStruct((seq_count, width // 2, 2 * width), F32),
        in_specs=[VMEM] * 3,
        out_specs=VMEM,
        scratch_shapes=[pltpu.VMEM((2 * width, width), F32)],
        compiler_params=params,
        name="weigh",
    )(inverse, packed, other)
    scores = pl.pallas_call(
        score,
        out_shape=jax.ShapeDtypeStruct((seq_count, queries.shape[0]), F32),
        in_specs=[VMEM] * 3,
        out_specs=VMEM,
        compiler_params=params,
        name="score",
    )(weights, swap(weights), queries)
    return scores.T


def solution(mesh):
    placed = (
        P(("groups", "seq"), "tensor"),
        P(("groups", "seq"), "tensor"),
        P("tensor", None),
        P("tensor", None),
        P(("groups", "seq", "tensor"), None),
        P("groups"),
    )
    return jax.shard_map(
        shards,
        mesh=mesh,
        in_specs=placed,
        out_specs=P(("groups", "seq", "tensor"), None),
        check_vma=False,
    )
```

```python
import functools
import math

import jax
import jax.numpy as jnp
from jax import lax
from jax.experimental import pallas as pl
from jax.experimental.pallas import tpu as pltpu
from jax.sharding import PartitionSpec as P

LEN = 512
DAMPING = 0.1
PANEL = 16
VMEM = pl.BlockSpec(memory_space=pltpu.VMEM)
HBM = pl.BlockSpec(memory_space=pltpu.HBM)
NN = (((1,), (0,)), ((), ()))
NT = (((1,), (1,)), ((), ()))
F32 = jnp.float32


def split(lo, hi, parts, unit):
    units = (hi - lo) // unit
    edges = [lo + unit * -(-units * part // parts) for part in range(parts + 1)]
    return list(zip(edges, edges[1:]))


def project(spans, lengths, inputs, grads, proj_in, proj_out, out, buf, count, sems):
    width, tokens = proj_in.shape[0], inputs.shape[0]
    tile = 2 * tokens
    outer = grads.shape[1]
    x_rows, g_rows = pl.ds(width, tokens), pl.ds(width + tokens, tokens)
    px_rows, pg_rows = pl.ds(0, width), pl.ds(width + tile, width)
    for part, (lo, hi) in enumerate(spans):
        cols = pl.ds(lo, hi - lo)
        for src, rows in ((proj_in, px_rows), (inputs, x_rows), (grads, g_rows), (proj_out, pg_rows)):
            if lo < src.shape[1]:
                pltpu.make_async_copy(src.at[:, cols], buf.at[rows, cols], sems.at[part]).start()
    scalars = pltpu.make_async_copy(lengths, count, sems.at[len(spans)])
    scalars.start()

    def multiply(*accs):
        step = 0
        for part, (lo, hi) in enumerate(spans):
            rows = buf.shape[0] if lo < outer else width + tokens
            landed = buf.at[pl.ds(0, rows), pl.ds(lo, hi - lo)]
            pltpu.make_async_copy(landed, landed, sems.at[part]).wait()
            tiles = [pl.ds(start, tile) for start in range(lo, hi, tile)]
            if lo < outer:
                pairs = [((x_rows, px_rows, cols), (g_rows, pg_rows, cols)) for cols in tiles]
            else:
                pairs = [tuple((x_rows, px_rows, cols) for cols in tiles[i : i + 2]) for i in range(0, len(tiles), 2)]
            for pair in pairs:
                unit, stage = step % 2, step // 2 % 2
                step += 1
                blocks = [buf[rows, cols] for rows, _, cols in pair]
                both = jnp.concatenate(blocks * (2 // len(blocks)), axis=0)
                pltpu.matmul_push_rhs(both, stage, unit, transpose=True)
                for place, (rows, mat_rows, cols) in enumerate(pair):
                    acc = accs[2 * (place + (place == 1 and rows is x_rows)) + unit]
                    pltpu.matmul_acc_lhs(acc, buf[mat_rows, cols], load_staged_rhs=None if place else stage)
        scalars.wait()
        first = lax.axis_index("seq") * tokens
        valid = lax.broadcasted_iota(jnp.int32, (width, tokens), 1) + first % LEN < count[first // LEN]
        x_left, g_right, x_right = (
            pltpu.matmul_pop(accs[2 * kind]) + pltpu.matmul_pop(accs[2 * kind + 1]) for kind in range(3)
        )
        out[:width, :] = jnp.where(valid, x_left[:, :tokens] + x_right[:, tokens:], 0.0)
        out[width:, :] = jnp.where(valid, g_right[:, tokens:], 0.0)

    pl.run_scoped(multiply, *(pltpu.ACC(mxu_id=unit)((width, tile), F32) for unit in (0, 1, 0, 1, 0, 1)))


def dot3(a, b, dims):
    halves = []
    for part in (a, b):
        high = part.astype(jnp.bfloat16)
        halves.append((high, (part - high.astype(F32)).astype(jnp.bfloat16)))
    (ah, al), (bh, bl) = halves
    dot = functools.partial(lax.dot_general, dimension_numbers=dims, preferred_element_type=F32)
    return dot(ah, bh) + (dot(ah, bl) + dot(al, bh))


def moments(mine, other, out):
    out[...] = jnp.zeros_like(out)

    @pl.when(lax.axis_index("tensor") == 1)
    def _():
        z = mine[...] + other[...]
        square = dot3(z, z, NT)
        width = square.shape[0] // 2
        top, bottom = square[:width], pltpu.roll(square[width:], width, 1)
        row = lax.broadcasted_iota(jnp.int32, top.shape, 0)
        lane = lax.broadcasted_iota(jnp.int32, top.shape, 1)
        out[0, :width] = jnp.where(lane < row, bottom, top)
        diagonal = jnp.sum(jnp.where(lane == row, bottom, 0.0), axis=0, keepdims=True)
        out[0, width : width + 1] = diagonal


def unpack(packed, diagonal):
    width = packed.shape[0]
    left = packed[:, :width]
    flipped = left.T
    row = lax.broadcasted_iota(jnp.int32, left.shape, 0)
    lane = lax.broadcasted_iota(jnp.int32, left.shape, 1)
    inner = jnp.where(lane < row, flipped, left)
    outer = jnp.where(lane < row, left, jnp.where(lane == row, diagonal[:, :width], flipped))
    return jnp.concatenate([inner, outer], axis=1)


def invert(state):
    width = state.shape[0]
    lane = lax.broadcasted_iota(jnp.int32, (8, 2 * width), 1)
    row_of = lax.broadcasted_iota(jnp.int32, (8, 2 * width), 0)
    column = lane % width
    right = lane - column

    def panel(step, carry):
        first = step * PANEL
        own = pl.ds(pl.multiple_of(first, PANEL), PANEL)
        inside = (column >= first) & (column < first + PANEL)
        index = [right + (first + t) for t in range(PANEL)]
        block = state[own, :]
        pivots = [block[8 * i : 8 * i + 8] for i in range(PANEL // 8)]
        heads = [[jnp.take_along_axis(p, index[t], axis=1) for p in pivots] for t in range(PANEL)]
        rows = [state[8 * b : 8 * b + 8, :] for b in range(width // 8)]
        cols = [[jnp.take_along_axis(r, index[t], axis=1) for r in rows] for t in range(PANEL)]
        for i in range(PANEL // 8):
            unit = jnp.where(column - first == row_of + 8 * i, 1.0, 0.0)
            pivots[i] = jnp.where(inside, unit, pivots[i])
        for t in range(PANEL):
            at, sub = t // 8, t % 8
            here = row_of == sub
            inverse = 1.0 / heads[t][at][sub : sub + 1]
            rest = [jnp.where(here, 0.0, h) if i == at else h for i, h in enumerate(heads[t])]

            def step_rows(tiles):
                scaled = tiles[at][sub : sub + 1] * inverse
                return [(jnp.where(here, scaled, x) if i == at else x) - rest[i] * scaled for i, x in enumerate(tiles)]

            pivots = step_rows(pivots)
            heads[t + 1 :] = [step_rows(head) for head in heads[t + 1 :]]
        for b in range(width // 8):
            total = jnp.where(inside, 0.0, rows[b])
            for t in range(PANEL):
                total = total - cols[t][b] * pivots[t // 8][t % 8 : t % 8 + 1]
            state[8 * b : 8 * b + 8, :] = total
        state[own, :] = jnp.concatenate(pivots, axis=0)
        return carry

    lax.fori_loop(0, width // PANEL, panel, 0)


def inverses(total, mine, other, out):
    @pl.when(lax.axis_index("tensor") == 1)
    def _():
        width = out.shape[0]
        packed = mine[0] + other[0]
        both = unpack(packed[:width], packed[width : width + 1])
        lane = lax.broadcasted_iota(jnp.int32, both.shape, 1)
        row = lax.broadcasted_iota(jnp.int32, both.shape, 0)
        out[...] = both * (1.0 / total) + jnp.where(lane % width == row, DAMPING, 0.0)
        invert(out)


def weigh(scaling, inv, mine, other, out):
    @pl.when(lax.axis_index("tensor") == 1)
    def _():
        slabs = mine.shape[0]
        width = inv.shape[0]
        half = width // 2
        left = lax.broadcasted_iota(jnp.int32, inv.shape, 1) < width
        rows = jnp.concatenate([inv[pl.ds(0, half, 2), :], inv[pl.ds(1, half, 2), :]], axis=0)
        inv_out = jnp.where(left, 0.0, rows * scaling)
        inv_in = inv[...]
        diagonal = jnp.concatenate(
            [jnp.where(left, inv_in, 0.0), jnp.where(left, 0.0, pltpu.roll(inv_in, width, 1))], axis=0
        )
        devices = lax.axis_size("seq")
        upper = lax.axis_index("seq") // (devices // 2) == 1
        for slab in range(slabs):
            first, second = mine[slab, :width], other[slab, :width]
            cross = jnp.concatenate([jnp.where(upper, second, first), jnp.where(upper, first, second)], axis=0)
            both = dot3(dot3(inv_out, cross, NT), diagonal, NN)
            even, odd = both[:half], both[half:]
            out[slab] = jnp.where(left[:half], even, pltpu.roll(odd, width, 1)).astype(out.dtype)
            out[slabs + slab] = jnp.where(left[:half], pltpu.roll(even, width, 1), odd).astype(out.dtype)


def score(mine, other, queries, out):
    is_weight = lax.axis_index("tensor") == 1
    count, chunks, lanes = mine.shape
    ones = jnp.ones((8, lanes), jnp.bfloat16)
    blocks = [queries[:, lanes * m : lanes * (m + 1)].astype(F32) for m in range(chunks)]
    for s in range(count):
        weights = jnp.where(is_weight, mine[s], other[s]).astype(F32)
        terms = [block * weights[m : m + 1] for m, block in enumerate(blocks)]
        while len(terms) > 1:
            terms = [x + y for x, y in zip(terms[::2], terms[1::2])]
        sums = terms[0]
        if sums.shape[0] == 1:
            out[s : s + 1, :] = jnp.sum(sums, axis=1, keepdims=True)
            continue
        total = 0.0
        for _ in range(3):
            part = sums.astype(jnp.bfloat16)
            sums = sums - part.astype(F32)
            total = total + lax.dot_general(ones, part, NT, preferred_element_type=F32)
        out[s : s + 1, :] = total[:1]


def stay(array):
    return pltpu.with_memory_space_constraint(array, pltpu.HBM)


def swap(array):
    return lax.ppermute(array, "tensor", [(0, 1), (1, 0)])


def exchange(array, distance, groups, devices):
    near = {1: 2, 2: 2, 3: 3}.get(distance, 1)
    pairs = []
    for chip in range(groups * devices):
        pairs.append((2 * chip, 2 * (chip ^ near)))
        pairs.append((2 * chip + 1, 2 * (chip ^ distance) + 1))
    return lax.ppermute(array, ("groups", "seq", "tensor"), pairs)


def gather(mine, other, distance, width):
    high = lax.axis_index("seq") // distance % 2 == 1
    both = jnp.stack([jnp.where(high, other, mine), jnp.where(high, mine, other)])
    left = jnp.arange(mine.shape[-1]) < width
    return jnp.where(left, mine + other, both).reshape((-1,) + mine.shape[1:])


def shards(inputs, out_grads, proj_in, proj_out, queries, lengths):
    width = proj_in.shape[1]
    tokens = inputs.shape[0]
    seq_count = lengths.shape[0]
    inner, outer = inputs.shape[1], out_grads.shape[1]
    tile = 2 * tokens
    spans = split(outer, inner, 1, 2 * tile) + split(0, outer, 3, tile)
    params = pltpu.CompilerParams(vmem_limit_bytes=16 << 20)
    partial_z = pl.pallas_call(
        functools.partial(project, spans),
        out_shape=jax.ShapeDtypeStruct((2 * width, tokens), F32),
        in_specs=[HBM] * 5,
        out_specs=VMEM,
        scratch_shapes=[
            pltpu.VMEM((2 * (width + tokens), inner), inputs.dtype),
            pltpu.SMEM(lengths.shape, lengths.dtype),
            pltpu.SemaphoreType.DMA((len(spans) + 1,)),
        ],
        compiler_params=params,
        name="project",
    )(*map(stay, (lengths, inputs, out_grads, proj_in.T, proj_out.T)))
    packed_rows = width + 8
    packed = pl.pallas_call(
        moments,
        out_shape=jax.ShapeDtypeStruct((1, packed_rows, 2 * width), F32),
        in_specs=[VMEM] * 2,
        out_specs=VMEM,
        compiler_params=params,
        name="moments",
    )(partial_z, swap(partial_z))
    groups, devices = lax.axis_size("groups"), lax.axis_size("seq")
    holders = devices // seq_count
    packed = packed + sum(exchange(packed, near, groups, devices) for near in range(1, holders))
    distance = holders
    while 2 * distance < devices:
        packed = gather(packed, exchange(packed, distance, groups, devices), distance, width)
        distance *= 2
    total = 3 * seq_count * LEN // 4
    scaling = 1.0 / (width * math.sqrt(LEN))
    other = exchange(packed, distance, groups, devices)
    inverse = pl.pallas_call(
        functools.partial(inverses, float(total)),
        out_shape=jax.ShapeDtypeStruct((width, 2 * width), F32),
        in_specs=[VMEM] * 2,
        out_specs=VMEM,
        compiler_params=params,
        name="inverses",
    )(packed, other)
    weights = pl.pallas_call(
        functools.partial(weigh, scaling),
        out_shape=jax.ShapeDtypeStruct((seq_count, width // 2, 2 * width), jnp.bfloat16),
        in_specs=[VMEM] * 3,
        out_specs=VMEM,
        compiler_params=params,
        name="weigh",
    )(inverse, packed, other)
    scores = pl.pallas_call(
        score,
        out_shape=jax.ShapeDtypeStruct((seq_count, queries.shape[0]), F32),
        in_specs=[VMEM] * 3,
        out_specs=VMEM,
        compiler_params=params,
        name="score",
    )(weights, swap(weights), queries)
    return scores.T


def solution(mesh):
    placed = (
        P(("groups", "seq"), "tensor"),
        P(("groups", "seq"), "tensor"),
        P("tensor", None),
        P("tensor", None),
        P(("groups", "seq", "tensor"), None),
        P("groups"),
    )
    return jax.shard_map(
        shards,
        mesh=mesh,
        in_specs=placed,
        out_specs=P(("groups", "seq", "tensor"), None),
        check_vma=False,
    )
```

```python
import functools
import math

import jax
import jax.numpy as jnp
from jax import lax
from jax.experimental import pallas as pl
from jax.experimental.pallas import tpu as pltpu
from jax.sharding import PartitionSpec as P

LEN = 512
DAMPING = 0.1
PANEL = 16
VMEM = pl.BlockSpec(memory_space=pltpu.VMEM)
HBM = pl.BlockSpec(memory_space=pltpu.HBM)
NN = (((1,), (0,)), ((), ()))
NT = (((1,), (1,)), ((), ()))
F32 = jnp.float32


def split(lo, hi, parts, unit):
    units = (hi - lo) // unit
    edges = [lo + unit * -(-units * part // parts) for part in range(parts + 1)]
    return list(zip(edges, edges[1:]))


def project(spans, lengths, inputs, grads, proj_in, proj_out, out, sent, buf, count, sems):
    width, tokens = proj_in.shape[0], inputs.shape[0]
    tile = 2 * tokens
    outer = grads.shape[1]
    x_rows, g_rows = pl.ds(width, tokens), pl.ds(width + tokens, tokens)
    px_rows, pg_rows = pl.ds(0, width), pl.ds(width + tile, width)
    for part, (lo, hi) in enumerate(spans):
        cols = pl.ds(lo, hi - lo)
        for src, rows in ((proj_in, px_rows), (inputs, x_rows), (grads, g_rows), (proj_out, pg_rows)):
            if lo < src.shape[1]:
                pltpu.make_async_copy(src.at[:, cols], buf.at[rows, cols], sems.at[part]).start()
    scalars = pltpu.make_async_copy(lengths, count, sems.at[len(spans)])
    scalars.start()

    def multiply(*accs):
        step = 0
        for part, (lo, hi) in enumerate(spans):
            rows = buf.shape[0] if lo < outer else width + tokens
            landed = buf.at[pl.ds(0, rows), pl.ds(lo, hi - lo)]
            pltpu.make_async_copy(landed, landed, sems.at[part]).wait()
            tiles = [pl.ds(start, tile) for start in range(lo, hi, tile)]
            if lo < outer:
                pairs = [((x_rows, px_rows, cols), (g_rows, pg_rows, cols)) for cols in tiles]
            else:
                pairs = [tuple((x_rows, px_rows, cols) for cols in tiles[i : i + 2]) for i in range(0, len(tiles), 2)]
            for pair in pairs:
                unit, stage = step % 2, step // 2 % 2
                step += 1
                blocks = [buf[rows, cols] for rows, _, cols in pair]
                both = jnp.concatenate(blocks * (2 // len(blocks)), axis=0)
                pltpu.matmul_push_rhs(both, stage, unit, transpose=True)
                for place, (rows, mat_rows, cols) in enumerate(pair):
                    acc = accs[2 * (place + (place == 1 and rows is x_rows)) + unit]
                    pltpu.matmul_acc_lhs(acc, buf[mat_rows, cols], load_staged_rhs=None if place else stage)
        scalars.wait()
        first = lax.axis_index("seq") * tokens
        valid = lax.broadcasted_iota(jnp.int32, (width, tokens), 1) + first % LEN < count[first // LEN]
        x_left, g_right, x_right = (
            pltpu.matmul_pop(accs[2 * kind]) + pltpu.matmul_pop(accs[2 * kind + 1]) for kind in range(3)
        )
        out[:width, :] = jnp.where(valid, x_left[:, :tokens] + x_right[:, tokens:], 0.0)
        out[width:, :] = jnp.where(valid, g_right[:, tokens:], 0.0)
        sent[...] = out[...].astype(sent.dtype)

    pl.run_scoped(multiply, *(pltpu.ACC(mxu_id=unit)((width, tile), F32) for unit in (0, 1, 0, 1, 0, 1)))


def dot3(a, b, dims):
    halves = []
    for part in (a, b):
        high = part.astype(jnp.bfloat16)
        halves.append((high, (part - high.astype(F32)).astype(jnp.bfloat16)))
    (ah, al), (bh, bl) = halves
    dot = functools.partial(lax.dot_general, dimension_numbers=dims, preferred_element_type=F32)
    return dot(ah, bh) + (dot(ah, bl) + dot(al, bh))


def moments(mine, other, out):
    out[...] = jnp.zeros_like(out)

    @pl.when(lax.axis_index("tensor") == 1)
    def _():
        z = mine[...] + other[...].astype(F32)
        z = z.astype(jnp.bfloat16)
        square = lax.dot_general(z, z, NT, preferred_element_type=F32)
        width = square.shape[0] // 2
        top, bottom = square[:width], pltpu.roll(square[width:], width, 1)
        row = lax.broadcasted_iota(jnp.int32, top.shape, 0)
        lane = lax.broadcasted_iota(jnp.int32, top.shape, 1)
        out[0, :width] = jnp.where(lane < row, bottom, top)
        diagonal = jnp.sum(jnp.where(lane == row, bottom, 0.0), axis=0, keepdims=True)
        out[0, width : width + 1] = diagonal


def unpack(packed, diagonal):
    width = packed.shape[0]
    left = packed[:, :width]
    flipped = left.T
    row = lax.broadcasted_iota(jnp.int32, left.shape, 0)
    lane = lax.broadcasted_iota(jnp.int32, left.shape, 1)
    inner = jnp.where(lane < row, flipped, left)
    outer = jnp.where(lane < row, left, jnp.where(lane == row, diagonal[:, :width], flipped))
    return jnp.concatenate([inner, outer], axis=1)


def invert(state):
    width = state.shape[0]
    lane = lax.broadcasted_iota(jnp.int32, (8, 2 * width), 1)
    row_of = lax.broadcasted_iota(jnp.int32, (8, 2 * width), 0)
    column = lane % width
    right = lane - column

    def panel(step, carry):
        first = step * PANEL
        own = pl.ds(pl.multiple_of(first, PANEL), PANEL)
        inside = (column >= first) & (column < first + PANEL)
        index = [right + (first + t) for t in range(PANEL)]
        block = state[own, :]
        pivots = [block[8 * i : 8 * i + 8] for i in range(PANEL // 8)]
        heads = [[jnp.take_along_axis(p, index[t], axis=1) for p in pivots] for t in range(PANEL)]
        rows = [state[8 * b : 8 * b + 8, :] for b in range(width // 8)]
        cols = [[jnp.take_along_axis(r, index[t], axis=1) for r in rows] for t in range(PANEL)]
        for i in range(PANEL // 8):
            unit = jnp.where(column - first == row_of + 8 * i, 1.0, 0.0)
            pivots[i] = jnp.where(inside, unit, pivots[i])
        for t in range(PANEL):
            at, sub = t // 8, t % 8
            here = row_of == sub
            inverse = 1.0 / heads[t][at][sub : sub + 1]
            rest = [jnp.where(here, 0.0, h) if i == at else h for i, h in enumerate(heads[t])]

            def step_rows(tiles):
                scaled = tiles[at][sub : sub + 1] * inverse
                return [(jnp.where(here, scaled, x) if i == at else x) - rest[i] * scaled for i, x in enumerate(tiles)]

            pivots = step_rows(pivots)
            heads[t + 1 :] = [step_rows(head) for head in heads[t + 1 :]]
        for b in range(width // 8):
            total = jnp.where(inside, 0.0, rows[b])
            for t in range(PANEL):
                total = total - cols[t][b] * pivots[t // 8][t % 8 : t % 8 + 1]
            state[8 * b : 8 * b + 8, :] = total
        state[own, :] = jnp.concatenate(pivots, axis=0)
        return carry

    lax.fori_loop(0, width // PANEL, panel, 0)


def inverses(total, mine, other, out):
    @pl.when(lax.axis_index("tensor") == 1)
    def _():
        width = out.shape[0]
        packed = mine[0] + other[0]
        both = unpack(packed[:width], packed[width : width + 1])
        lane = lax.broadcasted_iota(jnp.int32, both.shape, 1)
        row = lax.broadcasted_iota(jnp.int32, both.shape, 0)
        out[...] = both * (1.0 / total) + jnp.where(lane % width == row, DAMPING, 0.0)
        invert(out)


def weigh(scaling, inv, mine, other, out):
    @pl.when(lax.axis_index("tensor") == 1)
    def _():
        slabs = mine.shape[0]
        width = inv.shape[0]
        half = width // 2
        left = lax.broadcasted_iota(jnp.int32, inv.shape, 1) < width
        rows = jnp.concatenate([inv[pl.ds(0, half, 2), :], inv[pl.ds(1, half, 2), :]], axis=0)
        inv_out = jnp.where(left, 0.0, rows * scaling)
        inv_in = inv[...]
        diagonal = jnp.concatenate(
            [jnp.where(left, inv_in, 0.0), jnp.where(left, 0.0, pltpu.roll(inv_in, width, 1))], axis=0
        )
        devices = lax.axis_size("seq")
        upper = lax.axis_index("seq") // (devices // 2) == 1
        for slab in range(slabs):
            first, second = mine[slab, :width], other[slab, :width]
            cross = jnp.concatenate([jnp.where(upper, second, first), jnp.where(upper, first, second)], axis=0)
            both = dot3(dot3(inv_out, cross, NT), diagonal, NN)
            even, odd = both[:half], both[half:]
            out[slab] = jnp.where(left[:half], even, pltpu.roll(odd, width, 1)).astype(out.dtype)
            out[slabs + slab] = jnp.where(left[:half], pltpu.roll(even, width, 1), odd).astype(out.dtype)


def score(mine, other, queries, out):
    is_weight = lax.axis_index("tensor") == 1
    count, chunks, lanes = mine.shape
    ones = jnp.ones((8, lanes), jnp.bfloat16)
    blocks = [queries[:, lanes * m : lanes * (m + 1)].astype(F32) for m in range(chunks)]
    for s in range(count):
        weights = jnp.where(is_weight, mine[s], other[s]).astype(F32)
        terms = [block * weights[m : m + 1] for m, block in enumerate(blocks)]
        while len(terms) > 1:
            terms = [x + y for x, y in zip(terms[::2], terms[1::2])]
        sums = terms[0]
        if sums.shape[0] == 1:
            out[s : s + 1, :] = jnp.sum(sums, axis=1, keepdims=True)
            continue
        total = 0.0
        for _ in range(3):
            part = sums.astype(jnp.bfloat16)
            sums = sums - part.astype(F32)
            total = total + lax.dot_general(ones, part, NT, preferred_element_type=F32)
        out[s : s + 1, :] = total[:1]


def stay(array):
    return pltpu.with_memory_space_constraint(array, pltpu.HBM)


def swap(array):
    return lax.ppermute(array, "tensor", [(0, 1), (1, 0)])


def exchange(array, distance, groups, devices):
    near = {1: 2, 2: 2, 3: 3}.get(distance, 1)
    pairs = []
    for chip in range(groups * devices):
        pairs.append((2 * chip, 2 * (chip ^ near)))
        pairs.append((2 * chip + 1, 2 * (chip ^ distance) + 1))
    return lax.ppermute(array, ("groups", "seq", "tensor"), pairs)


def gather(mine, other, distance, width):
    high = lax.axis_index("seq") // distance % 2 == 1
    both = jnp.stack([jnp.where(high, other, mine), jnp.where(high, mine, other)])
    left = jnp.arange(mine.shape[-1]) < width
    return jnp.where(left, mine + other, both).reshape((-1,) + mine.shape[1:])


def shards(inputs, out_grads, proj_in, proj_out, queries, lengths):
    width = proj_in.shape[1]
    tokens = inputs.shape[0]
    seq_count = lengths.shape[0]
    inner, outer = inputs.shape[1], out_grads.shape[1]
    tile = 2 * tokens
    spans = split(outer, inner, 1, 2 * tile) + split(0, outer, 3, tile)
    params = pltpu.CompilerParams(vmem_limit_bytes=16 << 20)
    partial_z, sent = pl.pallas_call(
        functools.partial(project, spans),
        out_shape=[jax.ShapeDtypeStruct((2 * width, tokens), kind) for kind in (F32, jnp.bfloat16)],
        in_specs=[HBM] * 5,
        out_specs=[VMEM] * 2,
        scratch_shapes=[
            pltpu.VMEM((2 * (width + tokens), inner), inputs.dtype),
            pltpu.SMEM(lengths.shape, lengths.dtype),
            pltpu.SemaphoreType.DMA((len(spans) + 1,)),
        ],
        compiler_params=params,
        name="project",
    )(*map(stay, (lengths, inputs, out_grads, proj_in.T, proj_out.T)))
    packed_rows = width + 1
    packed = pl.pallas_call(
        moments,
        out_shape=jax.ShapeDtypeStruct((1, packed_rows, 2 * width), F32),
        in_specs=[VMEM] * 2,
        out_specs=VMEM,
        compiler_params=params,
        name="moments",
    )(partial_z, swap(sent))
    groups, devices = lax.axis_size("groups"), lax.axis_size("seq")
    holders = devices // seq_count
    packed = packed + sum(exchange(packed, near, groups, devices) for near in range(1, holders))
    distance = holders
    while 2 * distance < devices:
        packed = gather(packed, exchange(packed, distance, groups, devices), distance, width)
        distance *= 2
    total = 3 * seq_count * LEN // 4
    scaling = 1.0 / (width * math.sqrt(LEN))
    other = exchange(packed, distance, groups, devices)
    inverse = pl.pallas_call(
        functools.partial(inverses, float(total)),
        out_shape=jax.ShapeDtypeStruct((width, 2 * width), F32),
        in_specs=[VMEM] * 2,
        out_specs=VMEM,
        compiler_params=params,
        name="inverses",
    )(packed, other)
    weights = pl.pallas_call(
        functools.partial(weigh, scaling),
        out_shape=jax.ShapeDtypeStruct((seq_count, width // 2, 2 * width), jnp.bfloat16),
        in_specs=[VMEM] * 3,
        out_specs=VMEM,
        compiler_params=params,
        name="weigh",
    )(inverse, packed, other)
    scores = pl.pallas_call(
        score,
        out_shape=jax.ShapeDtypeStruct((seq_count, queries.shape[0]), F32),
        in_specs=[VMEM] * 3,
        out_specs=VMEM,
        compiler_params=params,
        name="score",
    )(weights, swap(weights), queries)
    return scores.T


def solution(mesh):
    placed = (
        P(("groups", "seq"), "tensor"),
        P(("groups", "seq"), "tensor"),
        P("tensor", None),
        P("tensor", None),
        P(("groups", "seq", "tensor"), None),
        P("groups"),
    )
    return jax.shard_map(
        shards,
        mesh=mesh,
        in_specs=placed,
        out_specs=P(("groups", "seq", "tensor"), None),
        check_vma=False,
    )
```

```python
import functools
import math

import jax
import jax.numpy as jnp
from jax import lax
from jax.experimental import pallas as pl
from jax.experimental.pallas import tpu as pltpu
from jax.sharding import PartitionSpec as P

LEN = 512
DAMPING = 0.1
PANEL = 16
VMEM = pl.BlockSpec(memory_space=pltpu.VMEM)
HBM = pl.BlockSpec(memory_space=pltpu.HBM)
NN = (((1,), (0,)), ((), ()))
NT = (((1,), (1,)), ((), ()))
F32 = jnp.float32


def split(lo, hi, parts, unit):
    units = (hi - lo) // unit
    edges = [lo + unit * -(-units * part // parts) for part in range(parts + 1)]
    return list(zip(edges, edges[1:]))


def project(spans, lengths, inputs, grads, proj_in, proj_out, out, sent, buf, count, sems):
    width, tokens = proj_in.shape[0], inputs.shape[0]
    tile = 2 * tokens
    outer = grads.shape[1]
    x_rows, g_rows = pl.ds(width, tokens), pl.ds(width + tokens, tokens)
    px_rows, pg_rows = pl.ds(0, width), pl.ds(width + tile, width)
    for part, (lo, hi) in enumerate(spans):
        cols = pl.ds(lo, hi - lo)
        for src, rows in ((proj_in, px_rows), (inputs, x_rows), (grads, g_rows), (proj_out, pg_rows)):
            if lo < src.shape[1]:
                pltpu.make_async_copy(src.at[:, cols], buf.at[rows, cols], sems.at[part]).start()
    scalars = pltpu.make_async_copy(lengths, count, sems.at[len(spans)])
    scalars.start()

    def multiply(*accs):
        step = 0
        for part, (lo, hi) in enumerate(spans):
            rows = buf.shape[0] if lo < outer else width + tokens
            landed = buf.at[pl.ds(0, rows), pl.ds(lo, hi - lo)]
            pltpu.make_async_copy(landed, landed, sems.at[part]).wait()
            tiles = [pl.ds(start, tile) for start in range(lo, hi, tile)]
            if lo < outer:
                pairs = [((x_rows, px_rows, cols), (g_rows, pg_rows, cols)) for cols in tiles]
            else:
                pairs = [tuple((x_rows, px_rows, cols) for cols in tiles[i : i + 2]) for i in range(0, len(tiles), 2)]
            for pair in pairs:
                unit, stage = step % 2, step // 2 % 2
                step += 1
                blocks = [buf[rows, cols] for rows, _, cols in pair]
                both = jnp.concatenate(blocks * (2 // len(blocks)), axis=0)
                pltpu.matmul_push_rhs(both, stage, unit, transpose=True)
                for place, (rows, mat_rows, cols) in enumerate(pair):
                    acc = accs[2 * (place + (place == 1 and rows is x_rows)) + unit]
                    pltpu.matmul_acc_lhs(acc, buf[mat_rows, cols], load_staged_rhs=None if place else stage)
        scalars.wait()
        first = lax.axis_index("seq") * tokens
        valid = lax.broadcasted_iota(jnp.int32, (width, tokens), 1) + first % LEN < count[first // LEN]
        x_left, g_right, x_right = (
            pltpu.matmul_pop(accs[2 * kind]) + pltpu.matmul_pop(accs[2 * kind + 1]) for kind in range(3)
        )
        out[:width, :] = jnp.where(valid, x_left[:, :tokens] + x_right[:, tokens:], 0.0)
        out[width:, :] = jnp.where(valid, g_right[:, tokens:], 0.0)
        sent[...] = out[...].astype(sent.dtype)

    pl.run_scoped(multiply, *(pltpu.ACC(mxu_id=unit)((width, tile), F32) for unit in (0, 1, 0, 1, 0, 1)))


def dot3(a, b, dims):
    halves = []
    for part in (a, b):
        high = part.astype(jnp.bfloat16)
        halves.append((high, (part - high.astype(F32)).astype(jnp.bfloat16)))
    (ah, al), (bh, bl) = halves
    dot = functools.partial(lax.dot_general, dimension_numbers=dims, preferred_element_type=F32)
    return dot(ah, bh) + (dot(ah, bl) + dot(al, bh))


def moments(mine, other, out):
    out[...] = jnp.zeros_like(out)

    @pl.when(lax.axis_index("tensor") == 1)
    def _():
        z = mine[...] + other[...].astype(F32)
        z = z.astype(jnp.bfloat16)
        square = lax.dot_general(z, z, NT, preferred_element_type=F32)
        width = square.shape[0] // 2
        top, bottom = square[:width], pltpu.roll(square[width:], width, 1)
        row = lax.broadcasted_iota(jnp.int32, top.shape, 0)
        lane = lax.broadcasted_iota(jnp.int32, top.shape, 1)
        out[0, :width] = jnp.where(lane < row, bottom, top)
        diagonal = jnp.sum(jnp.where(lane == row, bottom, 0.0), axis=0, keepdims=True)
        out[0, width : width + 1] = diagonal


def unpack(packed, diagonal):
    width = packed.shape[0]
    left = packed[:, :width]
    flipped = left.T
    row = lax.broadcasted_iota(jnp.int32, left.shape, 0)
    lane = lax.broadcasted_iota(jnp.int32, left.shape, 1)
    inner = jnp.where(lane < row, flipped, left)
    outer = jnp.where(lane < row, left, jnp.where(lane == row, diagonal[:, :width], flipped))
    return jnp.concatenate([inner, outer], axis=1)


def invert(state):
    width = state.shape[0]
    lane = lax.broadcasted_iota(jnp.int32, (8, 2 * width), 1)
    row_of = lax.broadcasted_iota(jnp.int32, (8, 2 * width), 0)
    column = lane % width
    right = lane - column

    def panel(step, carry):
        first = step * PANEL
        own = pl.ds(pl.multiple_of(first, PANEL), PANEL)
        inside = (column >= first) & (column < first + PANEL)
        index = [right + (first + t) for t in range(PANEL)]
        block = state[own, :]
        pivots = [block[8 * i : 8 * i + 8] for i in range(PANEL // 8)]
        heads = [[jnp.take_along_axis(p, index[t], axis=1) for p in pivots] for t in range(PANEL)]
        rows = [state[8 * b : 8 * b + 8, :] for b in range(width // 8)]
        cols = [[jnp.take_along_axis(r, index[t], axis=1) for r in rows] for t in range(PANEL)]
        for i in range(PANEL // 8):
            unit = jnp.where(column - first == row_of + 8 * i, 1.0, 0.0)
            pivots[i] = jnp.where(inside, unit, pivots[i])
        for t in range(PANEL):
            at, sub = t // 8, t % 8
            here = row_of == sub
            inverse = 1.0 / heads[t][at][sub : sub + 1]
            rest = [jnp.where(here, 0.0, h) if i == at else h for i, h in enumerate(heads[t])]

            def step_rows(tiles):
                scaled = tiles[at][sub : sub + 1] * inverse
                return [(jnp.where(here, scaled, x) if i == at else x) - rest[i] * scaled for i, x in enumerate(tiles)]

            pivots = step_rows(pivots)
            heads[t + 1 :] = [step_rows(head) for head in heads[t + 1 :]]
        for b in range(width // 8):
            total = jnp.where(inside, 0.0, rows[b])
            for t in range(PANEL):
                total = total - cols[t][b] * pivots[t // 8][t % 8 : t % 8 + 1]
            state[8 * b : 8 * b + 8, :] = total
        state[own, :] = jnp.concatenate(pivots, axis=0)
        return carry

    lax.fori_loop(0, width // PANEL, panel, 0)


def solve(total, scaling, mine, other, out, inv):
    inverses(total, mine, other, inv)
    weigh(scaling, inv, mine, other, out)


def inverses(total, mine, other, out):
    @pl.when(lax.axis_index("tensor") == 1)
    def _():
        width = out.shape[0]
        packed = mine[0] + other[0]
        both = unpack(packed[:width], packed[width : width + 1])
        lane = lax.broadcasted_iota(jnp.int32, both.shape, 1)
        row = lax.broadcasted_iota(jnp.int32, both.shape, 0)
        out[...] = both * (1.0 / total) + jnp.where(lane % width == row, DAMPING, 0.0)
        invert(out)


def weigh(scaling, inv, mine, other, out):
    @pl.when(lax.axis_index("tensor") == 1)
    def _():
        slabs = mine.shape[0]
        width = inv.shape[0]
        half = width // 2
        left = lax.broadcasted_iota(jnp.int32, inv.shape, 1) < width
        rows = jnp.concatenate([inv[pl.ds(0, half, 2), :], inv[pl.ds(1, half, 2), :]], axis=0)
        inv_out = jnp.where(left, 0.0, rows * scaling)
        inv_in = inv[...]
        diagonal = jnp.concatenate(
            [jnp.where(left, inv_in, 0.0), jnp.where(left, 0.0, pltpu.roll(inv_in, width, 1))], axis=0
        )
        devices = lax.axis_size("seq")
        upper = lax.axis_index("seq") // (devices // 2) == 1
        for slab in range(slabs):
            first, second = mine[slab, :width], other[slab, :width]
            cross = jnp.concatenate([jnp.where(upper, second, first), jnp.where(upper, first, second)], axis=0)
            both = dot3(dot3(inv_out, cross, NT), diagonal, NN)
            even, odd = both[:half], both[half:]
            out[slab] = jnp.where(left[:half], even, pltpu.roll(odd, width, 1)).astype(out.dtype)
            out[slabs + slab] = jnp.where(left[:half], pltpu.roll(even, width, 1), odd).astype(out.dtype)


def score(mine, other, queries, out):
    is_weight = lax.axis_index("tensor") == 1
    count, chunks, lanes = mine.shape
    ones = jnp.ones((8, lanes), jnp.bfloat16)
    blocks = [queries[:, lanes * m : lanes * (m + 1)].astype(F32) for m in range(chunks)]
    for s in range(count):
        weights = jnp.where(is_weight, mine[s], other[s]).astype(F32)
        terms = [block * weights[m : m + 1] for m, block in enumerate(blocks)]
        while len(terms) > 1:
            terms = [x + y for x, y in zip(terms[::2], terms[1::2])]
        sums = terms[0]
        if sums.shape[0] == 1:
            out[s : s + 1, :] = jnp.sum(sums, axis=1, keepdims=True)
            continue
        total = 0.0
        for _ in range(3):
            part = sums.astype(jnp.bfloat16)
            sums = sums - part.astype(F32)
            total = total + lax.dot_general(ones, part, NT, preferred_element_type=F32)
        out[s : s + 1, :] = total[:1]


def stay(array):
    return pltpu.with_memory_space_constraint(array, pltpu.HBM)


def swap(array):
    return lax.ppermute(array, "tensor", [(0, 1), (1, 0)])


def exchange(array, distance, groups, devices):
    near = {1: 2, 2: 2, 3: 3}.get(distance, 1)
    pairs = []
    for chip in range(groups * devices):
        pairs.append((2 * chip, 2 * (chip ^ near)))
        pairs.append((2 * chip + 1, 2 * (chip ^ distance) + 1))
    return lax.ppermute(array, ("groups", "seq", "tensor"), pairs)


def gather(mine, other, distance, width):
    high = lax.axis_index("seq") // distance % 2 == 1
    both = jnp.stack([jnp.where(high, other, mine), jnp.where(high, mine, other)])
    left = jnp.arange(mine.shape[-1]) < width
    return jnp.where(left, mine + other, both).reshape((-1,) + mine.shape[1:])


def shards(inputs, out_grads, proj_in, proj_out, queries, lengths):
    width = proj_in.shape[1]
    tokens = inputs.shape[0]
    seq_count = lengths.shape[0]
    inner, outer = inputs.shape[1], out_grads.shape[1]
    tile = 2 * tokens
    spans = split(outer, inner, 1, 2 * tile) + split(0, outer, 3, tile)
    params = pltpu.CompilerParams(vmem_limit_bytes=16 << 20)
    partial_z, sent = pl.pallas_call(
        functools.partial(project, spans),
        out_shape=[jax.ShapeDtypeStruct((2 * width, tokens), kind) for kind in (F32, jnp.bfloat16)],
        in_specs=[HBM] * 5,
        out_specs=[VMEM] * 2,
        scratch_shapes=[
            pltpu.VMEM((2 * (width + tokens), inner), inputs.dtype),
            pltpu.SMEM(lengths.shape, lengths.dtype),
            pltpu.SemaphoreType.DMA((len(spans) + 1,)),
        ],
        compiler_params=params,
        name="project",
    )(*map(stay, (lengths, inputs, out_grads, proj_in.T, proj_out.T)))
    packed_rows = width + 1
    packed = pl.pallas_call(
        moments,
        out_shape=jax.ShapeDtypeStruct((1, packed_rows, 2 * width), F32),
        in_specs=[VMEM] * 2,
        out_specs=VMEM,
        compiler_params=params,
        name="moments",
    )(partial_z, swap(sent))
    groups, devices = lax.axis_size("groups"), lax.axis_size("seq")
    holders = devices // seq_count
    packed = packed + sum(exchange(packed, near, groups, devices) for near in range(1, holders))
    distance = holders
    while 2 * distance < devices:
        packed = gather(packed, exchange(packed, distance, groups, devices), distance, width)
        distance *= 2
    total = 3 * seq_count * LEN // 4
    scaling = 1.0 / (width * math.sqrt(LEN))
    other = exchange(packed, distance, groups, devices)
    weights = pl.pallas_call(
        functools.partial(solve, float(total), scaling),
        out_shape=jax.ShapeDtypeStruct((seq_count, width // 2, 2 * width), jnp.bfloat16),
        in_specs=[VMEM] * 2,
        out_specs=VMEM,
        scratch_shapes=[pltpu.VMEM((width, 2 * width), F32)],
        compiler_params=params,
        name="solve",
    )(packed, other)
    scores = pl.pallas_call(
        score,
        out_shape=jax.ShapeDtypeStruct((seq_count, queries.shape[0]), F32),
        in_specs=[VMEM] * 3,
        out_specs=VMEM,
        compiler_params=params,
        name="score",
    )(weights, swap(weights), queries)
    return scores.T


def solution(mesh):
    placed = (
        P(("groups", "seq"), "tensor"),
        P(("groups", "seq"), "tensor"),
        P("tensor", None),
        P("tensor", None),
        P(("groups", "seq", "tensor"), None),
        P("groups"),
    )
    return jax.shard_map(
        shards,
        mesh=mesh,
        in_specs=placed,
        out_specs=P(("groups", "seq", "tensor"), None),
        check_vma=False,
    )
```

```python
import functools
import math

import jax
import jax.numpy as jnp
from jax import lax
from jax.experimental import pallas as pl
from jax.experimental.pallas import tpu as pltpu
from jax.sharding import PartitionSpec as P

LEN = 512
DAMPING = 0.1
PANEL = 16
VMEM = pl.BlockSpec(memory_space=pltpu.VMEM)
HBM = pl.BlockSpec(memory_space=pltpu.HBM)
NN = (((1,), (0,)), ((), ()))
NT = (((1,), (1,)), ((), ()))
F32 = jnp.float32


def split(lo, hi, parts, unit):
    units = (hi - lo) // unit
    edges = [lo + unit * -(-units * part // parts) for part in range(parts + 1)]
    return list(zip(edges, edges[1:]))


def project(spans, lengths, inputs, grads, proj_in, proj_out, out, sent, buf, count, sems):
    width, tokens = proj_in.shape[0], inputs.shape[0]
    tile = 2 * tokens
    outer = grads.shape[1]
    x_rows, g_rows = pl.ds(width, tokens), pl.ds(width + tokens, tokens)
    px_rows, pg_rows = pl.ds(0, width), pl.ds(width + tile, width)
    for part, (lo, hi) in enumerate(spans):
        cols = pl.ds(lo, hi - lo)
        for src, rows in ((proj_in, px_rows), (inputs, x_rows), (grads, g_rows), (proj_out, pg_rows)):
            if lo < src.shape[1]:
                pltpu.make_async_copy(src.at[:, cols], buf.at[rows, cols], sems.at[part]).start()
    scalars = pltpu.make_async_copy(lengths, count, sems.at[len(spans)])
    scalars.start()

    def multiply(*accs):
        step = 0
        for part, (lo, hi) in enumerate(spans):
            rows = buf.shape[0] if lo < outer else width + tokens
            landed = buf.at[pl.ds(0, rows), pl.ds(lo, hi - lo)]
            pltpu.make_async_copy(landed, landed, sems.at[part]).wait()
            tiles = [pl.ds(start, tile) for start in range(lo, hi, tile)]
            if lo < outer:
                pairs = [((x_rows, px_rows, cols), (g_rows, pg_rows, cols)) for cols in tiles]
            else:
                pairs = [tuple((x_rows, px_rows, cols) for cols in tiles[i : i + 2]) for i in range(0, len(tiles), 2)]
            for pair in pairs:
                unit, stage = step % 2, step // 2 % 2
                step += 1
                blocks = [buf[rows, cols] for rows, _, cols in pair]
                both = jnp.concatenate(blocks * (2 // len(blocks)), axis=0)
                pltpu.matmul_push_rhs(both, stage, unit, transpose=True)
                for place, (rows, mat_rows, cols) in enumerate(pair):
                    acc = accs[2 * (place + (place == 1 and rows is x_rows)) + unit]
                    pltpu.matmul_acc_lhs(acc, buf[mat_rows, cols], load_staged_rhs=None if place else stage)
        scalars.wait()
        first = lax.axis_index("seq") * tokens
        valid = lax.broadcasted_iota(jnp.int32, (width, tokens), 1) + first % LEN < count[first // LEN]
        x_left, g_right, x_right = (
            pltpu.matmul_pop(accs[2 * kind]) + pltpu.matmul_pop(accs[2 * kind + 1]) for kind in range(3)
        )
        out[:width, :] = jnp.where(valid, x_left[:, :tokens] + x_right[:, tokens:], 0.0)
        out[width:, :] = jnp.where(valid, g_right[:, tokens:], 0.0)
        sent[...] = out[...].astype(sent.dtype)

    pl.run_scoped(multiply, *(pltpu.ACC(mxu_id=unit)((width, tile), F32) for unit in (0, 1, 0, 1, 0, 1)))


def dot3(a, b, dims):
    halves = []
    for part in (a, b):
        high = part.astype(jnp.bfloat16)
        halves.append((high, (part - high.astype(F32)).astype(jnp.bfloat16)))
    (ah, al), (bh, bl) = halves
    dot = functools.partial(lax.dot_general, dimension_numbers=dims, preferred_element_type=F32)
    return dot(ah, bh) + (dot(ah, bl) + dot(al, bh))


def moments(mine, other, out):
    out[...] = jnp.zeros_like(out)

    @pl.when(lax.axis_index("tensor") == 1)
    def _():
        z = mine[...] + other[...].astype(F32)
        z = z.astype(jnp.bfloat16)
        square = lax.dot_general(z, z, NT, preferred_element_type=F32)
        width = square.shape[0] // 2
        top, bottom = square[:width], pltpu.roll(square[width:], width, 1)
        row = lax.broadcasted_iota(jnp.int32, top.shape, 0)
        lane = lax.broadcasted_iota(jnp.int32, top.shape, 1)
        out[0, :width] = jnp.where(lane < row, bottom, top)
        diagonal = jnp.sum(jnp.where(lane == row, bottom, 0.0), axis=0, keepdims=True)
        out[0, width : width + 1] = diagonal


def unpack(packed, diagonal):
    width = packed.shape[0]
    left = packed[:, :width]
    flipped = left.T
    row = lax.broadcasted_iota(jnp.int32, left.shape, 0)
    lane = lax.broadcasted_iota(jnp.int32, left.shape, 1)
    inner = jnp.where(lane < row, flipped, left)
    outer = jnp.where(lane < row, left, jnp.where(lane == row, diagonal[:, :width], flipped))
    return jnp.concatenate([inner, outer], axis=1)


def invert(state):
    width = state.shape[0]
    lane = lax.broadcasted_iota(jnp.int32, (8, 2 * width), 1)
    row_of = lax.broadcasted_iota(jnp.int32, (8, 2 * width), 0)
    column = lane % width
    right = lane - column

    def panel(step, carry):
        first = step * PANEL
        own = pl.ds(pl.multiple_of(first, PANEL), PANEL)
        inside = (column >= first) & (column < first + PANEL)
        index = [right + (first + t) for t in range(PANEL)]
        block = state[own, :]
        pivots = [block[8 * i : 8 * i + 8] for i in range(PANEL // 8)]
        heads = [[jnp.take_along_axis(p, index[t], axis=1) for p in pivots] for t in range(PANEL)]
        rows = [state[8 * b : 8 * b + 8, :] for b in range(width // 8)]
        cols = [[jnp.take_along_axis(r, index[t], axis=1) for r in rows] for t in range(PANEL)]
        for i in range(PANEL // 8):
            unit = jnp.where(column - first == row_of + 8 * i, 1.0, 0.0)
            pivots[i] = jnp.where(inside, unit, pivots[i])
        for t in range(PANEL):
            at, sub = t // 8, t % 8
            here = row_of == sub
            inverse = 1.0 / heads[t][at][sub : sub + 1]
            rest = [jnp.where(here, 0.0, h) if i == at else h for i, h in enumerate(heads[t])]

            def step_rows(tiles):
                scaled = tiles[at][sub : sub + 1] * inverse
                return [(jnp.where(here, scaled, x) if i == at else x) - rest[i] * scaled for i, x in enumerate(tiles)]

            pivots = step_rows(pivots)
            heads[t + 1 :] = [step_rows(head) for head in heads[t + 1 :]]
        for b in range(width // 8):
            total = jnp.where(inside, 0.0, rows[b])
            for t in range(PANEL):
                total = total - cols[t][b] * pivots[t // 8][t % 8 : t % 8 + 1]
            state[8 * b : 8 * b + 8, :] = total
        state[own, :] = jnp.concatenate(pivots, axis=0)
        return carry

    lax.fori_loop(0, width // PANEL, panel, 0)


def inverses(total, mine, other, out):
    @pl.when(lax.axis_index("tensor") == 1)
    def _():
        width = out.shape[0]
        packed = mine[0] + other[0]
        both = unpack(packed[:width], packed[width : width + 1])
        lane = lax.broadcasted_iota(jnp.int32, both.shape, 1)
        row = lax.broadcasted_iota(jnp.int32, both.shape, 0)
        out[...] = both * (1.0 / total) + jnp.where(lane % width == row, DAMPING, 0.0)
        invert(out)


def weigh(scaling, inv, mine, other, out):
    @pl.when(lax.axis_index("tensor") == 1)
    def _():
        slabs = mine.shape[0]
        width = inv.shape[0]
        half = width // 2
        left = lax.broadcasted_iota(jnp.int32, inv.shape, 1) < width
        rows = jnp.concatenate([inv[pl.ds(0, half, 2), :], inv[pl.ds(1, half, 2), :]], axis=0)
        inv_out = jnp.where(left, 0.0, rows * scaling)
        inv_in = inv[...]
        diagonal = jnp.concatenate(
            [jnp.where(left, inv_in, 0.0), jnp.where(left, 0.0, pltpu.roll(inv_in, width, 1))], axis=0
        )
        devices = lax.axis_size("seq")
        upper = lax.axis_index("seq") // (devices // 2) == 1
        for slab in range(slabs):
            first, second = mine[slab, :width], other[slab, :width]
            cross = jnp.concatenate([jnp.where(upper, second, first), jnp.where(upper, first, second)], axis=0)
            both = dot3(dot3(inv_out, cross, NT), diagonal, NN)
            even, odd = both[:half], both[half:]
            out[slab] = jnp.where(left[:half], even, pltpu.roll(odd, width, 1)).astype(out.dtype)
            out[slabs + slab] = jnp.where(left[:half], pltpu.roll(even, width, 1), odd).astype(out.dtype)


def score(mine, other, queries, out):
    is_weight = lax.axis_index("tensor") == 1
    count, chunks, lanes = mine.shape
    ones = jnp.ones((8, lanes), jnp.bfloat16)
    blocks = [queries[:, lanes * m : lanes * (m + 1)].astype(F32) for m in range(chunks)]
    for s in range(count):
        weights = jnp.where(is_weight, mine[s], other[s]).astype(F32)
        terms = [block * weights[m : m + 1] for m, block in enumerate(blocks)]
        while len(terms) > 1:
            terms = [x + y for x, y in zip(terms[::2], terms[1::2])]
        sums = terms[0]
        if sums.shape[0] == 1:
            out[s : s + 1, :] = jnp.sum(sums, axis=1, keepdims=True)
            continue
        total = 0.0
        for _ in range(2):
            part = sums.astype(jnp.bfloat16)
            sums = sums - part.astype(F32)
            total = total + lax.dot_general(ones, part, NT, preferred_element_type=F32)
        out[s : s + 1, :] = total[:1]


def stay(array):
    return pltpu.with_memory_space_constraint(array, pltpu.HBM)


def swap(array):
    return lax.ppermute(array, "tensor", [(0, 1), (1, 0)])


def exchange(array, distance, groups, devices):
    near = {1: 2, 2: 2, 3: 3}.get(distance, 1)
    pairs = []
    for chip in range(groups * devices):
        pairs.append((2 * chip, 2 * (chip ^ near)))
        pairs.append((2 * chip + 1, 2 * (chip ^ distance) + 1))
    return lax.ppermute(array, ("groups", "seq", "tensor"), pairs)


def gather(mine, other, distance, width):
    high = lax.axis_index("seq") // distance % 2 == 1
    both = jnp.stack([jnp.where(high, other, mine), jnp.where(high, mine, other)])
    left = jnp.arange(mine.shape[-1]) < width
    return jnp.where(left, mine + other, both).reshape((-1,) + mine.shape[1:])


def shards(inputs, out_grads, proj_in, proj_out, queries, lengths):
    width = proj_in.shape[1]
    tokens = inputs.shape[0]
    seq_count = lengths.shape[0]
    inner, outer = inputs.shape[1], out_grads.shape[1]
    tile = 2 * tokens
    spans = split(outer, inner, 1, 2 * tile) + split(0, outer, 3, tile)
    params = pltpu.CompilerParams(vmem_limit_bytes=16 << 20)
    partial_z, sent = pl.pallas_call(
        functools.partial(project, spans),
        out_shape=[jax.ShapeDtypeStruct((2 * width, tokens), kind) for kind in (F32, jnp.bfloat16)],
        in_specs=[HBM] * 5,
        out_specs=[VMEM] * 2,
        scratch_shapes=[
            pltpu.VMEM((2 * (width + tokens), inner), inputs.dtype),
            pltpu.SMEM(lengths.shape, lengths.dtype),
            pltpu.SemaphoreType.DMA((len(spans) + 1,)),
        ],
        compiler_params=params,
        name="project",
    )(*map(stay, (lengths, inputs, out_grads, proj_in.T, proj_out.T)))
    packed_rows = width + 1
    packed = pl.pallas_call(
        moments,
        out_shape=jax.ShapeDtypeStruct((1, packed_rows, 2 * width), F32),
        in_specs=[VMEM] * 2,
        out_specs=VMEM,
        compiler_params=params,
        name="moments",
    )(partial_z, swap(sent))
    groups, devices = lax.axis_size("groups"), lax.axis_size("seq")
    holders = devices // seq_count
    packed = packed + sum(exchange(packed, near, groups, devices) for near in range(1, holders))
    distance = holders
    while 2 * distance < devices:
        packed = gather(packed, exchange(packed, distance, groups, devices), distance, width)
        distance *= 2
    total = 3 * seq_count * LEN // 4
    scaling = 1.0 / (width * math.sqrt(LEN))
    other = exchange(packed, distance, groups, devices)
    inverse = pl.pallas_call(
        functools.partial(inverses, float(total)),
        out_shape=jax.ShapeDtypeStruct((width, 2 * width), F32),
        in_specs=[VMEM] * 2,
        out_specs=VMEM,
        compiler_params=params,
        name="inverses",
    )(packed, other)
    weights = pl.pallas_call(
        functools.partial(weigh, scaling),
        out_shape=jax.ShapeDtypeStruct((seq_count, width // 2, 2 * width), jnp.bfloat16),
        in_specs=[VMEM] * 3,
        out_specs=VMEM,
        compiler_params=params,
        name="weigh",
    )(inverse, packed, other)
    scores = pl.pallas_call(
        score,
        out_shape=jax.ShapeDtypeStruct((seq_count, queries.shape[0]), F32),
        in_specs=[VMEM] * 3,
        out_specs=VMEM,
        compiler_params=params,
        name="score",
    )(weights, swap(weights), queries)
    return scores.T


def solution(mesh):
    placed = (
        P(("groups", "seq"), "tensor"),
        P(("groups", "seq"), "tensor"),
        P("tensor", None),
        P("tensor", None),
        P(("groups", "seq", "tensor"), None),
        P("groups"),
    )
    return jax.shard_map(
        shards,
        mesh=mesh,
        in_specs=placed,
        out_specs=P(("groups", "seq", "tensor"), None),
        check_vma=False,
    )
```

```python
import functools
import math

import jax
import jax.numpy as jnp
from jax import lax
from jax.experimental import pallas as pl
from jax.experimental.pallas import tpu as pltpu
from jax.sharding import PartitionSpec as P

LEN = 512
DAMPING = 0.1
PANEL = 16
VMEM = pl.BlockSpec(memory_space=pltpu.VMEM)
HBM = pl.BlockSpec(memory_space=pltpu.HBM)
NN = (((1,), (0,)), ((), ()))
NT = (((1,), (1,)), ((), ()))
F32 = jnp.float32


def split(lo, hi, parts, unit):
    units = (hi - lo) // unit
    edges = [lo + unit * -(-units * part // parts) for part in range(parts + 1)]
    return list(zip(edges, edges[1:]))


def project(spans, lengths, inputs, grads, proj_in, proj_out, out, sent, buf, count, sems):
    width, tokens = proj_in.shape[0], inputs.shape[0]
    tile = 2 * tokens
    outer = grads.shape[1]
    x_rows, g_rows = pl.ds(width, tokens), pl.ds(width + tokens, tokens)
    px_rows, pg_rows = pl.ds(0, width), pl.ds(width + tile, width)
    for part, (lo, hi) in enumerate(spans):
        cols = pl.ds(lo, hi - lo)
        for src, rows in ((proj_in, px_rows), (inputs, x_rows), (grads, g_rows), (proj_out, pg_rows)):
            if lo < src.shape[1]:
                pltpu.make_async_copy(src.at[:, cols], buf.at[rows, cols], sems.at[part]).start()
    scalars = pltpu.make_async_copy(lengths, count, sems.at[len(spans)])
    scalars.start()

    def multiply(*accs):
        step = 0
        for part, (lo, hi) in enumerate(spans):
            rows = buf.shape[0] if lo < outer else width + tokens
            landed = buf.at[pl.ds(0, rows), pl.ds(lo, hi - lo)]
            pltpu.make_async_copy(landed, landed, sems.at[part]).wait()
            tiles = [pl.ds(start, tile) for start in range(lo, hi, tile)]
            if lo < outer:
                pairs = [((x_rows, px_rows, cols), (g_rows, pg_rows, cols)) for cols in tiles]
            else:
                pairs = [tuple((x_rows, px_rows, cols) for cols in tiles[i : i + 2]) for i in range(0, len(tiles), 2)]
            for pair in pairs:
                unit, stage = step % 2, step // 2 % 2
                step += 1
                blocks = [buf[rows, cols] for rows, _, cols in pair]
                both = jnp.concatenate(blocks * (2 // len(blocks)), axis=0)
                pltpu.matmul_push_rhs(both, stage, unit, transpose=True)
                for place, (rows, mat_rows, cols) in enumerate(pair):
                    acc = accs[2 * (place + (place == 1 and rows is x_rows)) + unit]
                    pltpu.matmul_acc_lhs(acc, buf[mat_rows, cols], load_staged_rhs=None if place else stage)
        scalars.wait()
        first = lax.axis_index("seq") * tokens
        valid = lax.broadcasted_iota(jnp.int32, (width, tokens), 1) + first % LEN < count[first // LEN]
        x_left, g_right, x_right = (
            pltpu.matmul_pop(accs[2 * kind]) + pltpu.matmul_pop(accs[2 * kind + 1]) for kind in range(3)
        )
        out[:width, :] = jnp.where(valid, x_left[:, :tokens] + x_right[:, tokens:], 0.0)
        out[width:, :] = jnp.where(valid, g_right[:, tokens:], 0.0)
        sent[...] = out[...].astype(sent.dtype)

    pl.run_scoped(multiply, *(pltpu.ACC(mxu_id=unit)((width, tile), F32) for unit in (0, 1, 0, 1, 0, 1)))


def dot3(a, b, dims):
    halves = []
    for part in (a, b):
        high = part.astype(jnp.bfloat16)
        halves.append((high, (part - high.astype(F32)).astype(jnp.bfloat16)))
    (ah, al), (bh, bl) = halves
    dot = functools.partial(lax.dot_general, dimension_numbers=dims, preferred_element_type=F32)
    return dot(ah, bh) + (dot(ah, bl) + dot(al, bh))


def moments(mine, other, out):
    out[...] = jnp.zeros_like(out)

    @pl.when(lax.axis_index("tensor") == 1)
    def _():
        z = mine[...] + other[...].astype(F32)
        z = z.astype(jnp.bfloat16)
        square = lax.dot_general(z, z, NT, preferred_element_type=F32)
        width = square.shape[0] // 2
        top, bottom = square[:width], pltpu.roll(square[width:], width, 1)
        row = lax.broadcasted_iota(jnp.int32, top.shape, 0)
        lane = lax.broadcasted_iota(jnp.int32, top.shape, 1)
        out[0, :width] = jnp.where(lane < row, bottom, top)
        diagonal = jnp.sum(jnp.where(lane == row, bottom, 0.0), axis=0, keepdims=True)
        out[0, width : width + 1] = diagonal


def unpack(packed, diagonal):
    width = packed.shape[0]
    left = packed[:, :width]
    flipped = left.T
    row = lax.broadcasted_iota(jnp.int32, left.shape, 0)
    lane = lax.broadcasted_iota(jnp.int32, left.shape, 1)
    inner = jnp.where(lane < row, flipped, left)
    outer = jnp.where(lane < row, left, jnp.where(lane == row, diagonal[:, :width], flipped))
    return jnp.concatenate([inner, outer], axis=1)


def invert(state):
    width = state.shape[0]
    lane = lax.broadcasted_iota(jnp.int32, (8, 2 * width), 1)
    row_of = lax.broadcasted_iota(jnp.int32, (8, 2 * width), 0)
    column = lane % width
    right = lane - column

    def panel(step, carry):
        first = step * PANEL
        own = pl.ds(pl.multiple_of(first, PANEL), PANEL)
        inside = (column >= first) & (column < first + PANEL)
        index = [right + (first + t) for t in range(PANEL)]
        block = state[own, :]
        pivots = [block[8 * i : 8 * i + 8] for i in range(PANEL // 8)]
        heads = [[jnp.take_along_axis(p, index[t], axis=1) for p in pivots] for t in range(PANEL)]
        rows = [state[8 * b : 8 * b + 8, :] for b in range(width // 8)]
        cols = [[jnp.take_along_axis(r, index[t], axis=1) for r in rows] for t in range(PANEL)]
        for i in range(PANEL // 8):
            unit = jnp.where(column - first == row_of + 8 * i, 1.0, 0.0)
            pivots[i] = jnp.where(inside, unit, pivots[i])
        for t in range(PANEL):
            at, sub = t // 8, t % 8
            here = row_of == sub
            inverse = 1.0 / heads[t][at][sub : sub + 1]
            rest = [jnp.where(here, 0.0, h) if i == at else h for i, h in enumerate(heads[t])]

            def step_rows(tiles):
                scaled = tiles[at][sub : sub + 1] * inverse
                return [(jnp.where(here, scaled, x) if i == at else x) - rest[i] * scaled for i, x in enumerate(tiles)]

            pivots = step_rows(pivots)
            heads[t + 1 :] = [step_rows(head) for head in heads[t + 1 :]]
        for b in range(width // 8):
            total = jnp.where(inside, 0.0, rows[b])
            for t in range(PANEL):
                total = total - cols[t][b] * pivots[t // 8][t % 8 : t % 8 + 1]
            state[8 * b : 8 * b + 8, :] = total
        state[own, :] = jnp.concatenate(pivots, axis=0)
        return carry

    lax.fori_loop(0, width // PANEL, panel, 0)


def inverses(total, mine, other, out):
    @pl.when(lax.axis_index("tensor") == 1)
    def _():
        width = out.shape[0]
        packed = mine[0] + other[0]
        both = unpack(packed[:width], packed[width : width + 1])
        lane = lax.broadcasted_iota(jnp.int32, both.shape, 1)
        row = lax.broadcasted_iota(jnp.int32, both.shape, 0)
        out[...] = both * (1.0 / total) + jnp.where(lane % width == row, DAMPING, 0.0)
        invert(out)


def weigh(scaling, inv, mine, other, out):
    @pl.when(lax.axis_index("tensor") == 1)
    def _():
        slabs = mine.shape[0]
        width = inv.shape[0]
        half = width // 2
        left = lax.broadcasted_iota(jnp.int32, inv.shape, 1) < width
        rows = jnp.concatenate([inv[pl.ds(0, half, 2), :], inv[pl.ds(1, half, 2), :]], axis=0)
        inv_out = jnp.where(left, 0.0, rows * scaling)
        inv_in = inv[...]
        diagonal = jnp.concatenate(
            [jnp.where(left, inv_in, 0.0), jnp.where(left, 0.0, pltpu.roll(inv_in, width, 1))], axis=0
        )
        devices = lax.axis_size("seq")
        upper = lax.axis_index("seq") // (devices // 2) == 1
        for slab in range(slabs):
            first, second = mine[slab, :width], other[slab, :width]
            cross = jnp.concatenate([jnp.where(upper, second, first), jnp.where(upper, first, second)], axis=0)
            both = dot3(dot3(inv_out, cross, NT), diagonal, NN)
            even, odd = both[:half], both[half:]
            out[slab] = jnp.where(left[:half], even, pltpu.roll(odd, width, 1)).astype(out.dtype)
            out[slabs + slab] = jnp.where(left[:half], pltpu.roll(even, width, 1), odd).astype(out.dtype)


def score(mine, other, queries, out):
    is_weight = lax.axis_index("tensor") == 1
    count, chunks, lanes = mine.shape
    ones = jnp.ones((8, lanes), jnp.bfloat16)
    blocks = [queries[:, lanes * m : lanes * (m + 1)].astype(F32) for m in range(chunks)]
    for s in range(count):
        weights = jnp.where(is_weight, mine[s], other[s]).astype(F32)
        terms = [block * weights[m : m + 1] for m, block in enumerate(blocks)]
        while len(terms) > 1:
            terms = [x + y for x, y in zip(terms[::2], terms[1::2])]
        sums = terms[0]
        if sums.shape[0] == 1:
            out[s : s + 1, :] = jnp.sum(sums, axis=1, keepdims=True)
            continue
        total = 0.0
        for _ in range(3):
            part = sums.astype(jnp.bfloat16)
            sums = sums - part.astype(F32)
            total = total + lax.dot_general(ones, part, NT, preferred_element_type=F32)
        out[s : s + 1, :] = total[:1]


def stay(array):
    return pltpu.with_memory_space_constraint(array, pltpu.HBM)


def swap(array):
    return lax.ppermute(array, "tensor", [(0, 1), (1, 0)])


def exchange(array, distance, groups, devices):
    near = {1: devices, 2: devices, 3: 2}.get(distance, 1)
    pairs = []
    for chip in range(groups * devices):
        pairs.append((2 * chip, 2 * (chip ^ near)))
        pairs.append((2 * chip + 1, 2 * (chip ^ distance) + 1))
    return lax.ppermute(array, ("groups", "seq", "tensor"), pairs)


def gather(mine, other, distance, width):
    high = lax.axis_index("seq") // distance % 2 == 1
    both = jnp.stack([jnp.where(high, other, mine), jnp.where(high, mine, other)])
    left = jnp.arange(mine.shape[-1]) < width
    return jnp.where(left, mine + other, both).reshape((-1,) + mine.shape[1:])


def shards(inputs, out_grads, proj_in, proj_out, queries, lengths):
    width = proj_in.shape[1]
    tokens = inputs.shape[0]
    seq_count = lengths.shape[0]
    inner, outer = inputs.shape[1], out_grads.shape[1]
    tile = 2 * tokens
    spans = split(outer, inner, 1, 2 * tile) + split(0, outer, 3, tile)
    params = pltpu.CompilerParams(vmem_limit_bytes=16 << 20)
    partial_z, sent = pl.pallas_call(
        functools.partial(project, spans),
        out_shape=[jax.ShapeDtypeStruct((2 * width, tokens), kind) for kind in (F32, jnp.bfloat16)],
        in_specs=[HBM] * 5,
        out_specs=[VMEM] * 2,
        scratch_shapes=[
            pltpu.VMEM((2 * (width + tokens), inner), inputs.dtype),
            pltpu.SMEM(lengths.shape, lengths.dtype),
            pltpu.SemaphoreType.DMA((len(spans) + 1,)),
        ],
        compiler_params=params,
        name="project",
    )(*map(stay, (lengths, inputs, out_grads, proj_in.T, proj_out.T)))
    packed_rows = width + 1
    packed = pl.pallas_call(
        moments,
        out_shape=jax.ShapeDtypeStruct((1, packed_rows, 2 * width), F32),
        in_specs=[VMEM] * 2,
        out_specs=VMEM,
        compiler_params=params,
        name="moments",
    )(partial_z, swap(sent))
    groups, devices = lax.axis_size("groups"), lax.axis_size("seq")
    holders = devices // seq_count
    packed = packed + sum(exchange(packed, near, groups, devices) for near in range(1, holders))
    distance = holders
    while 2 * distance < devices:
        packed = gather(packed, exchange(packed, distance, groups, devices), distance, width)
        distance *= 2
    total = 3 * seq_count * LEN // 4
    scaling = 1.0 / (width * math.sqrt(LEN))
    other = exchange(packed, distance, groups, devices)
    inverse = pl.pallas_call(
        functools.partial(inverses, float(total)),
        out_shape=jax.ShapeDtypeStruct((width, 2 * width), F32),
        in_specs=[VMEM] * 2,
        out_specs=VMEM,
        compiler_params=params,
        name="inverses",
    )(packed, other)
    weights = pl.pallas_call(
        functools.partial(weigh, scaling),
        out_shape=jax.ShapeDtypeStruct((seq_count, width // 2, 2 * width), jnp.bfloat16),
        in_specs=[VMEM] * 3,
        out_specs=VMEM,
        compiler_params=params,
        name="weigh",
    )(inverse, packed, other)
    scores = pl.pallas_call(
        score,
        out_shape=jax.ShapeDtypeStruct((seq_count, queries.shape[0]), F32),
        in_specs=[VMEM] * 3,
        out_specs=VMEM,
        compiler_params=params,
        name="score",
    )(weights, swap(weights), queries)
    return scores.T


def solution(mesh):
    placed = (
        P(("groups", "seq"), "tensor"),
        P(("groups", "seq"), "tensor"),
        P("tensor", None),
        P("tensor", None),
        P(("groups", "seq", "tensor"), None),
        P("groups"),
    )
    return jax.shard_map(
        shards,
        mesh=mesh,
        in_specs=placed,
        out_specs=P(("groups", "seq", "tensor"), None),
        check_vma=False,
    )
```

```python
import functools
import math

import jax
import jax.numpy as jnp
from jax import lax
from jax.experimental import pallas as pl
from jax.experimental.pallas import tpu as pltpu
from jax.sharding import PartitionSpec as P

LEN = 512
DAMPING = 0.1
PANEL = 16
VMEM = pl.BlockSpec(memory_space=pltpu.VMEM)
HBM = pl.BlockSpec(memory_space=pltpu.HBM)
NN = (((1,), (0,)), ((), ()))
NT = (((1,), (1,)), ((), ()))
F32 = jnp.float32


def split(lo, hi, parts, unit):
    units = (hi - lo) // unit
    edges = [lo + unit * -(-units * part // parts) for part in range(parts + 1)]
    return list(zip(edges, edges[1:]))


def project(spans, lengths, inputs, grads, proj_in, proj_out, out, buf, count, sems):
    width, tokens = proj_in.shape[0], inputs.shape[0]
    tile = 2 * tokens
    outer = grads.shape[1]
    x_rows, g_rows = pl.ds(width, tokens), pl.ds(width + tokens, tokens)
    px_rows, pg_rows = pl.ds(0, width), pl.ds(width + tile, width)
    for part, (lo, hi) in enumerate(spans):
        cols = pl.ds(lo, hi - lo)
        for src, rows in ((proj_in, px_rows), (inputs, x_rows), (grads, g_rows), (proj_out, pg_rows)):
            if lo < src.shape[1]:
                pltpu.make_async_copy(src.at[:, cols], buf.at[rows, cols], sems.at[part]).start()
    scalars = pltpu.make_async_copy(lengths, count, sems.at[len(spans)])
    scalars.start()

    def multiply(*accs):
        step = 0
        for part, (lo, hi) in enumerate(spans):
            rows = buf.shape[0] if lo < outer else width + tokens
            landed = buf.at[pl.ds(0, rows), pl.ds(lo, hi - lo)]
            pltpu.make_async_copy(landed, landed, sems.at[part]).wait()
            tiles = [pl.ds(start, tile) for start in range(lo, hi, tile)]
            if lo < outer:
                pairs = [((x_rows, px_rows, cols), (g_rows, pg_rows, cols)) for cols in tiles]
            else:
                pairs = [tuple((x_rows, px_rows, cols) for cols in tiles[i : i + 2]) for i in range(0, len(tiles), 2)]
            for pair in pairs:
                unit, stage = step % 2, step // 2 % 2
                step += 1
                blocks = [buf[rows, cols] for rows, _, cols in pair]
                both = jnp.concatenate(blocks * (2 // len(blocks)), axis=0)
                pltpu.matmul_push_rhs(both, stage, unit, transpose=True)
                for place, (rows, mat_rows, cols) in enumerate(pair):
                    acc = accs[2 * (place + (place == 1 and rows is x_rows)) + unit]
                    pltpu.matmul_acc_lhs(acc, buf[mat_rows, cols], load_staged_rhs=None if place else stage)
        scalars.wait()
        first = lax.axis_index("seq") * tokens
        valid = lax.broadcasted_iota(jnp.int32, (width, tokens), 1) + first % LEN < count[first // LEN]
        x_left, g_right, x_right = (
            pltpu.matmul_pop(accs[2 * kind]) + pltpu.matmul_pop(accs[2 * kind + 1]) for kind in range(3)
        )
        out[:width, :] = jnp.where(valid, x_left[:, :tokens] + x_right[:, tokens:], 0.0).astype(out.dtype)
        out[width:, :] = jnp.where(valid, g_right[:, tokens:], 0.0).astype(out.dtype)

    pl.run_scoped(multiply, *(pltpu.ACC(mxu_id=unit)((width, tile), F32) for unit in (0, 1, 0, 1, 0, 1)))


def dot3(a, b, dims):
    halves = []
    for part in (a, b):
        high = part.astype(jnp.bfloat16)
        halves.append((high, (part - high.astype(F32)).astype(jnp.bfloat16)))
    (ah, al), (bh, bl) = halves
    dot = functools.partial(lax.dot_general, dimension_numbers=dims, preferred_element_type=F32)
    return dot(ah, bh) + (dot(ah, bl) + dot(al, bh))


def moments(mine, other, out):
    out[...] = jnp.zeros_like(out)

    @pl.when(lax.axis_index("tensor") == 1)
    def _():
        z = mine[...].astype(F32) + other[...].astype(F32)
        zb = z.astype(jnp.bfloat16)
        square = lax.dot_general(zb, zb, NT, preferred_element_type=F32)
        width = square.shape[0] // 2
        top, bottom = square[:width], pltpu.roll(square[width:], width, 1)
        row = lax.broadcasted_iota(jnp.int32, top.shape, 0)
        lane = lax.broadcasted_iota(jnp.int32, top.shape, 1)
        out[0, :width] = jnp.where(lane < row, bottom, top)
        diagonal = jnp.sum(jnp.where(lane == row, bottom, 0.0), axis=0, keepdims=True)
        out[0, width : width + 1] = diagonal


def unpack(packed, diagonal):
    width = packed.shape[0]
    left = packed[:, :width]
    flipped = left.T
    row = lax.broadcasted_iota(jnp.int32, left.shape, 0)
    lane = lax.broadcasted_iota(jnp.int32, left.shape, 1)
    inner = jnp.where(lane < row, flipped, left)
    outer = jnp.where(lane < row, left, jnp.where(lane == row, diagonal[:, :width], flipped))
    return jnp.concatenate([inner, outer], axis=1)


def invert(state):
    width = state.shape[0]
    lane = lax.broadcasted_iota(jnp.int32, (8, 2 * width), 1)
    row_of = lax.broadcasted_iota(jnp.int32, (8, 2 * width), 0)
    column = lane % width
    right = lane - column

    def panel(step, carry):
        first = step * PANEL
        own = pl.ds(pl.multiple_of(first, PANEL), PANEL)
        inside = (column >= first) & (column < first + PANEL)
        index = [right + (first + t) for t in range(PANEL)]
        block = state[own, :]
        pivots = [block[8 * i : 8 * i + 8] for i in range(PANEL // 8)]
        heads = [[jnp.take_along_axis(p, index[t], axis=1) for p in pivots] for t in range(PANEL)]
        rows = [state[8 * b : 8 * b + 8, :] for b in range(width // 8)]
        cols = [[jnp.take_along_axis(r, index[t], axis=1) for r in rows] for t in range(PANEL)]
        for i in range(PANEL // 8):
            unit = jnp.where(column - first == row_of + 8 * i, 1.0, 0.0)
            pivots[i] = jnp.where(inside, unit, pivots[i])
        for t in range(PANEL):
            at, sub = t // 8, t % 8
            here = row_of == sub
            inverse = 1.0 / heads[t][at][sub : sub + 1]
            rest = [jnp.where(here, 0.0, h) if i == at else h for i, h in enumerate(heads[t])]

            def step_rows(tiles):
                scaled = tiles[at][sub : sub + 1] * inverse
                return [(jnp.where(here, scaled, x) if i == at else x) - rest[i] * scaled for i, x in enumerate(tiles)]

            pivots = step_rows(pivots)
            heads[t + 1 :] = [step_rows(head) for head in heads[t + 1 :]]
        for b in range(width // 8):
            total = jnp.where(inside, 0.0, rows[b])
            for t in range(PANEL):
                total = total - cols[t][b] * pivots[t // 8][t % 8 : t % 8 + 1]
            state[8 * b : 8 * b + 8, :] = total
        state[own, :] = jnp.concatenate(pivots, axis=0)
        return carry

    lax.fori_loop(0, width // PANEL, panel, 0)


def inverses(total, mine, other, out):
    @pl.when(lax.axis_index("tensor") == 1)
    def _():
        width = out.shape[0]
        packed = mine[0] + other[0]
        both = unpack(packed[:width], packed[width : width + 1])
        lane = lax.broadcasted_iota(jnp.int32, both.shape, 1)
        row = lax.broadcasted_iota(jnp.int32, both.shape, 0)
        out[...] = both * (1.0 / total) + jnp.where(lane % width == row, DAMPING, 0.0)
        invert(out)


def weigh(scaling, inv, mine, other, out):
    @pl.when(lax.axis_index("tensor") == 1)
    def _():
        slabs = mine.shape[0]
        width = inv.shape[0]
        half = width // 2
        left = lax.broadcasted_iota(jnp.int32, inv.shape, 1) < width
        rows = jnp.concatenate([inv[pl.ds(0, half, 2), :], inv[pl.ds(1, half, 2), :]], axis=0)
        inv_out = jnp.where(left, 0.0, rows * scaling)
        inv_in = inv[...]
        diagonal = jnp.concatenate(
            [jnp.where(left, inv_in, 0.0), jnp.where(left, 0.0, pltpu.roll(inv_in, width, 1))], axis=0
        )
        devices = lax.axis_size("seq")
        upper = lax.axis_index("seq") // (devices // 2) == 1
        for slab in range(slabs):
            first, second = mine[slab, :width], other[slab, :width]
            cross = jnp.concatenate([jnp.where(upper, second, first), jnp.where(upper, first, second)], axis=0)
            both = dot3(dot3(inv_out, cross, NT), diagonal, NN)
            even, odd = both[:half], both[half:]
            out[slab] = jnp.where(left[:half], even, pltpu.roll(odd, width, 1)).astype(out.dtype)
            out[slabs + slab] = jnp.where(left[:half], pltpu.roll(even, width, 1), odd).astype(out.dtype)


def score(mine, other, queries, out):
    is_weight = lax.axis_index("tensor") == 1
    count, chunks, lanes = mine.shape
    ones = jnp.ones((8, lanes), jnp.bfloat16)
    blocks = [queries[:, lanes * m : lanes * (m + 1)].astype(F32) for m in range(chunks)]
    for s in range(count):
        weights = jnp.where(is_weight, mine[s], other[s]).astype(F32)
        terms = [block * weights[m : m + 1] for m, block in enumerate(blocks)]
        while len(terms) > 1:
            terms = [x + y for x, y in zip(terms[::2], terms[1::2])]
        sums = terms[0]
        if sums.shape[0] == 1:
            out[s : s + 1, :] = jnp.sum(sums, axis=1, keepdims=True)
            continue
        total = 0.0
        for _ in range(3):
            part = sums.astype(jnp.bfloat16)
            sums = sums - part.astype(F32)
            total = total + lax.dot_general(ones, part, NT, preferred_element_type=F32)
        out[s : s + 1, :] = total[:1]


def stay(array):
    return pltpu.with_memory_space_constraint(array, pltpu.HBM)


def swap(array):
    return lax.ppermute(array, "tensor", [(0, 1), (1, 0)])


def exchange(array, distance, groups, devices):
    near = {1: 2, 2: 2, 3: 3}.get(distance, 1)
    pairs = []
    for chip in range(groups * devices):
        pairs.append((2 * chip, 2 * (chip ^ near)))
        pairs.append((2 * chip + 1, 2 * (chip ^ distance) + 1))
    return lax.ppermute(array, ("groups", "seq", "tensor"), pairs)


def gather(mine, other, distance, width):
    high = lax.axis_index("seq") // distance % 2 == 1
    both = jnp.stack([jnp.where(high, other, mine), jnp.where(high, mine, other)])
    left = jnp.arange(mine.shape[-1]) < width
    return jnp.where(left, mine + other, both).reshape((-1,) + mine.shape[1:])


def shards(inputs, out_grads, proj_in, proj_out, queries, lengths):
    width = proj_in.shape[1]
    tokens = inputs.shape[0]
    seq_count = lengths.shape[0]
    inner, outer = inputs.shape[1], out_grads.shape[1]
    tile = 2 * tokens
    spans = split(outer, inner, 1, 2 * tile) + split(0, outer, 3, tile)
    params = pltpu.CompilerParams(vmem_limit_bytes=16 << 20)
    partial_z = pl.pallas_call(
        functools.partial(project, spans),
        out_shape=jax.ShapeDtypeStruct((2 * width, tokens), jnp.bfloat16),
        in_specs=[HBM] * 5,
        out_specs=VMEM,
        scratch_shapes=[
            pltpu.VMEM((2 * (width + tokens), inner), inputs.dtype),
            pltpu.SMEM(lengths.shape, lengths.dtype),
            pltpu.SemaphoreType.DMA((len(spans) + 1,)),
        ],
        compiler_params=params,
        name="project",
    )(*map(stay, (lengths, inputs, out_grads, proj_in.T, proj_out.T)))
    packed_rows = width + 1
    packed = pl.pallas_call(
        moments,
        out_shape=jax.ShapeDtypeStruct((1, packed_rows, 2 * width), F32),
        in_specs=[VMEM] * 2,
        out_specs=VMEM,
        compiler_params=params,
        name="moments",
    )(partial_z, swap(partial_z))
    groups, devices = lax.axis_size("groups"), lax.axis_size("seq")
    holders = devices // seq_count
    packed = packed + sum(exchange(packed, near, groups, devices) for near in range(1, holders))
    distance = holders
    while 2 * distance < devices:
        packed = gather(packed, exchange(packed, distance, groups, devices), distance, width)
        distance *= 2
    total = 3 * seq_count * LEN // 4
    scaling = 1.0 / (width * math.sqrt(LEN))
    other = exchange(packed, distance, groups, devices)
    inverse = pl.pallas_call(
        functools.partial(inverses, float(total)),
        out_shape=jax.ShapeDtypeStruct((width, 2 * width), F32),
        in_specs=[VMEM] * 2,
        out_specs=VMEM,
        compiler_params=params,
        name="inverses",
    )(packed, other)
    weights = pl.pallas_call(
        functools.partial(weigh, scaling),
        out_shape=jax.ShapeDtypeStruct((seq_count, width // 2, 2 * width), jnp.bfloat16),
        in_specs=[VMEM] * 3,
        out_specs=VMEM,
        compiler_params=params,
        name="weigh",
    )(inverse, packed, other)
    scores = pl.pallas_call(
        score,
        out_shape=jax.ShapeDtypeStruct((seq_count, queries.shape[0]), F32),
        in_specs=[VMEM] * 3,
        out_specs=VMEM,
        compiler_params=params,
        name="score",
    )(weights, swap(weights), queries)
    return scores.T


def solution(mesh):
    placed = (
        P(("groups", "seq"), "tensor"),
        P(("groups", "seq"), "tensor"),
        P("tensor", None),
        P("tensor", None),
        P(("groups", "seq", "tensor"), None),
        P("groups"),
    )
    return jax.shard_map(
        shards,
        mesh=mesh,
        in_specs=placed,
        out_specs=P(("groups", "seq", "tensor"), None),
        check_vma=False,
    )
```
